256 devices in a mesh: clip: 8 (over x_lo, y), group: 32 (over x_hi, z, core).
Axes of the slice: x: 4 (x_hi: 2, x_lo: 2; x = x_hi * 2 + x_lo), y: 4, z: 8, core: 2. Of those that a mesh axis runs over, the one named last changes fastest.
Arguments:
- latents: bfloat16 [512, 640, 640], P(('clip', 'group')), may hold values from -8 to 8
- timestep: int32 [1], replicated, may hold values from 0 to 999
- context_frame: int32 [256], P(('clip', 'group')), may hold values from 0 to 1
- gain_pre: float32 [640], replicated, may hold values from 0.5 to 1.5
- w_temporal: bfloat16 [3, 640, 640], replicated, may hold values from -0.125 to 0.125
- w_time: float32 [640, 640], replicated, may hold values from -0.25 to 0.25
- gain_mid: float32 [640], replicated, may hold values from 0.5 to 1.5
- w_query: bfloat16 [640, 640], replicated, may hold values from -2 to 2
- w_key: bfloat16 [640, 640], replicated, may hold values from -2 to 2
- w_value: bfloat16 [640, 640], replicated, may hold values from -0.25 to 0.25
- w_out: bfloat16 [640, 640], replicated, may hold values from -1 to 1
Outputs:
- block_out: bfloat16 [512, 640, 640], P(('clip', 'group'))
The draws below stay inside these ranges and needn't reach their ends.
All inputs are finite; a program needn't handle non-finite values.
Results may differ from the reference program's by a relative error of at most 0.035.
Values may be sent and summed in bfloat16 or wider, within the bound.
No kernel may reach another device: no remote copies, remote signals or barrier semaphores. Data moves between devices by JAX's collectives and lax.ppermute only.
A program may use at most 128 MiB of HBM per device.

```python
import math
import jax
import jax.numpy as jnp
from jax import lax

C = 640
HEAD_DIM = 64
HEADS = 10
PH = 32
PW = 20
PIX = 640
F_DEV = 2
FRAMES = 512
N_CLIP = 8
N_GROUP = 32


def draw_latents(key, part):
    key = jax.random.fold_in(key, 3)
    first, second = jax.random.split(key)
    base = jax.random.normal(first, (FRAMES, PIX, C), jnp.float32)
    region_key, frame_key = jax.random.split(second)
    region = jax.random.normal(region_key, (FRAMES, 2, 1, 2, 1, C), jnp.float32) * 1.2
    spread = jnp.broadcast_to(region, (FRAMES, 2, PH // 2, 2, PW // 2, C)).reshape(FRAMES, PIX, C)
    whole = jax.random.normal(frame_key, (FRAMES, 1, C), jnp.float32) * 0.8
    values = base + spread + whole
    return jnp.clip(values, -8.0, 8.0).astype(jnp.bfloat16)


def draw_w_query(key, part):
    key = jax.random.fold_in(key, 11)
    own = jax.random.normal(key, (C, C), jnp.float32) / math.sqrt(C)
    values = own
    return jnp.clip(values, -2.0, 2.0).astype(jnp.bfloat16)


def draw_w_key(key, part):
    key = jax.random.fold_in(key, 12)
    own = jax.random.normal(key, (C, C), jnp.float32) / math.sqrt(C)
    values = 4.0 * own
    return jnp.clip(values, -2.0, 2.0).astype(jnp.bfloat16)


def place_ends(result, rng, least, largest):
    longest = result.shape.index(max(result.shape))
    spots = []
    for shift in (0, 1):
        where = [jax.random.randint(jax.random.fold_in(rng, axis), (), 0, length) for axis, length in enumerate(result.shape)]
        where[longest] = (where[longest] + shift) % result.shape[longest]
        spots.append(tuple(where))
    return result.at[spots[0]].set(least).at[spots[1]].set(largest)


def scatter_about(rng, shape, scale, limit, kind=jnp.bfloat16):
    drawn = scale * jax.random.normal(rng, shape, jnp.float32)
    return jnp.clip(drawn, min=-limit, max=limit).astype(kind)


def setup_inputs(seed: int = 0) -> dict:
    splits = jax.random.split(jax.random.key(seed), 12)
    return {
        "latents": draw_latents(jax.random.fold_in(splits[11], 71), 0),
        "timestep": jax.random.randint(splits[1], (1,), 0, 1000).astype(jnp.int32),
        "context_frame": place_ends(jax.random.randint(splits[2], (N_CLIP * N_GROUP,), 0, F_DEV), jax.random.fold_in(splits[2], 1), 0, F_DEV - 1).astype(jnp.int32),
        "gain_pre": jnp.clip(1.0 + 0.1 * jax.random.normal(splits[3], (C,), jnp.float32), 0.5, 1.5),
        "w_temporal": scatter_about(splits[4], (3, C, C), (3 * C) ** -0.5, 0.125),
        "w_time": scatter_about(splits[5], (C, C), C ** -0.5, 0.25, jnp.float32),
        "gain_mid": jnp.clip(1.0 + 0.1 * jax.random.normal(splits[6], (C,), jnp.float32), 0.5, 1.5),
        "w_query": draw_w_query(jax.random.fold_in(splits[11], 71), 0),
        "w_key": draw_w_key(jax.random.fold_in(splits[11], 71), 0),
        "w_value": scatter_about(splits[9], (C, C), C ** -0.5, 0.25),
        "w_out": scatter_about(splits[10], (C, C), (C // 16) ** -0.5, 1.0),
    }


def normalize(values, gain):
    return values * lax.rsqrt(lax.optimization_barrier(jnp.mean(values * values, -1, keepdims=True)) + 1e-06) * gain

def time_bias(timestep, w_time):
    half = w_time.shape[0] // 2
    freqs = jnp.exp(-math.log(10000.0) * jnp.arange(half, dtype=jnp.float32) / half)
    angle = timestep.astype(jnp.float32)[0] * freqs
    embed = jnp.concatenate([jnp.cos(angle), jnp.sin(angle)])
    return jnp.dot(jax.nn.silu(embed)[None, :], w_time, precision=lax.Precision.HIGHEST, preferred_element_type=jnp.float32)[0]

def project(left, weight):
    flat = left.reshape(-1, left.shape[-1])
    return jnp.dot(flat, weight, preferred_element_type=jnp.float32).reshape(left.shape[:-1] + (weight.shape[1],))

def pool_frame(frame):
    values = frame.astype(jnp.float32).reshape(2, PH // 2, 2, PW // 2, C)
    pooled = lax.optimization_barrier(jnp.mean(values, axis=(1, 3))).reshape(4, C)
    return normalize(pooled, 1.0).astype(jnp.bfloat16)

def attend(queries, keys, values):
    rows = queries.shape[0]
    qh = queries.astype(jnp.float32).reshape(rows, HEADS, HEAD_DIM)
    kh = keys.astype(jnp.float32).reshape(-1, HEADS, HEAD_DIM)
    vh = values.astype(jnp.float32).reshape(-1, HEADS, HEAD_DIM)
    scores = jnp.einsum('qhd,rhd->qhr', qh, kh) * 0.125
    peak = lax.optimization_barrier(jnp.max(scores, -1, keepdims=True))
    weights = jnp.exp(scores - peak)
    total = lax.optimization_barrier(jnp.sum(weights, -1))
    rounded = lax.optimization_barrier(weights.astype(jnp.bfloat16))
    summed = jnp.einsum('qhr,rhd->qhd', rounded.astype(jnp.float32), vh)
    return (summed / total[..., None]).reshape(rows, C).astype(jnp.bfloat16)

def reference(latents, timestep, context_frame, gain_pre, w_temporal, w_time, gain_mid, w_query, w_key, w_value, w_out):
    source = latents.astype(jnp.float32)
    norm1 = normalize(source, gain_pre).astype(jnp.bfloat16)
    before = jnp.roll(norm1, 1, 0)
    after = jnp.roll(norm1, -1, 0)
    temb = time_bias(timestep, w_time)
    conv = project(before, w_temporal[0]) + project(norm1, w_temporal[1]) + project(after, w_temporal[2])
    hidden = (source + conv + temb).astype(jnp.bfloat16)
    norm2 = normalize(hidden.astype(jnp.float32), gain_mid).astype(jnp.bfloat16)
    blocks = norm2.shape[0] // F_DEV
    chosen_index = (jnp.arange(blocks, dtype=jnp.int32) * F_DEV + context_frame.astype(jnp.int32)).astype(jnp.int32)
    chosen = norm2[chosen_index]
    ctx = jax.vmap(pool_frame)(chosen).reshape(-1, C)
    keys = jnp.dot(ctx, w_key, preferred_element_type=jnp.float32).astype(jnp.bfloat16)
    values = jnp.dot(ctx, w_value, preferred_element_type=jnp.float32).astype(jnp.bfloat16)

    def one_frame(pair):
        frame_hidden, frame_norm = pair
        queries = jnp.dot(frame_norm, w_query, preferred_element_type=jnp.float32).astype(jnp.bfloat16)
        attended = attend(queries, keys, values)
        mixed = frame_hidden.astype(jnp.float32) + jnp.dot(attended, w_out, preferred_element_type=jnp.float32)
        return mixed.astype(jnp.bfloat16)
    return lax.map(one_frame, (hidden, norm2))
```

```python
import math

import jax
import jax.numpy as jnp
from jax import lax
from jax.sharding import PartitionSpec as P

HEAD_DIM = 64
PH = 32
PW = 20


def padded_2(shard, sides, width):
    for axis, dim in sides:
        size, length = (lax.axis_size(axis), shard.shape[dim])
        up = [(i, (i + 1) % size) for i in range(size)]
        down = [(j, i) for i, j in up]
        last = lax.slice_in_dim(shard, length - width, length, axis=dim)
        first = lax.slice_in_dim(shard, 0, width, axis=dim)
        before = lax.ppermute(last, axis, up)
        after = lax.ppermute(first, axis, down)
        shard = jnp.concatenate([before, shard, after], axis=dim)
    return shard


AXES = ("clip", "group")


def place(device):
    clip, group = divmod(device, 32)
    x_low, y = divmod(clip, 4)
    x_high, rest = divmod(group, 16)
    z, core = divmod(rest, 2)
    return x_high * 2 + x_low, y, z, core


def groups_by(key):
    found = {}
    for device in range(256):
        found.setdefault(key(*place(device)), []).append(device)
    return list(found.values())


def spread(rows, groups):
    count = len(groups[0])
    copies = jnp.broadcast_to(rows[None], (count,) + rows.shape)
    got = lax.all_to_all(copies, AXES, 0, 0, axis_index_groups=groups, tiled=False)
    return got.reshape(count * rows.shape[0], rows.shape[1])


def gather_rows(rows):
    rows = spread(rows, groups_by(lambda x, y, z, core: (x, y, core)))
    rows = spread(rows, groups_by(lambda x, y, z, core: (z, core)))
    other = lax.ppermute(rows, AXES, [(i, i ^ 1) for i in range(256)])
    return jnp.concatenate([rows, other], axis=0)


def normalize(values, gain):
    return values * lax.rsqrt(jnp.mean(values * values, -1, keepdims=True) + 1e-06) * gain


def time_bias(timestep, w_time):
    half = w_time.shape[0] // 2
    freqs = jnp.exp(-math.log(10000.0) * jnp.arange(half, dtype=jnp.float32) / half)
    angle = timestep.astype(jnp.float32)[0] * freqs
    embed = jnp.concatenate([jnp.cos(angle), jnp.sin(angle)])
    return jnp.dot(
        jax.nn.silu(embed)[None, :],
        w_time,
        precision=lax.Precision.HIGHEST,
        preferred_element_type=jnp.float32,
    )[0]


def shards(
    latents,
    timestep,
    context_frame,
    gain_pre,
    w_temporal,
    w_time,
    gain_mid,
    w_query,
    w_key,
    w_value,
    w_out,
):
    frames, pixels, width = latents.shape
    heads = width // HEAD_DIM
    source = latents.astype(jnp.float32)
    norm1 = normalize(source, gain_pre).astype(jnp.bfloat16)
    padded = padded_2(norm1, ((("clip", "group"), 0),), 1)
    conv = jnp.zeros((frames * pixels, width), jnp.float32)
    for offset in range(3):
        window = padded[offset : offset + frames].reshape(frames * pixels, width)
        conv = conv + jnp.dot(window, w_temporal[offset], preferred_element_type=jnp.float32)
    temb = time_bias(timestep, w_time)
    hidden = (source + conv.reshape(frames, pixels, width) + temb).astype(jnp.bfloat16)
    norm2 = normalize(hidden.astype(jnp.float32), gain_mid).astype(jnp.bfloat16)
    chosen = lax.dynamic_index_in_dim(norm2, context_frame[0], 0, keepdims=False)
    regions = chosen.astype(jnp.float32).reshape(2, PH // 2, 2, PW // 2, width)
    pooled = jnp.mean(regions, axis=(1, 3)).reshape(4, width)
    ctx = normalize(pooled, 1.0).astype(jnp.bfloat16)
    all_ctx = gather_rows(ctx)
    all_keys = jnp.dot(all_ctx, w_key, preferred_element_type=jnp.float32).astype(jnp.bfloat16)
    all_values = jnp.dot(all_ctx, w_value, preferred_element_type=jnp.float32).astype(jnp.bfloat16)
    key_heads = all_keys.reshape(-1, heads, HEAD_DIM)
    value_heads = all_values.reshape(-1, heads, HEAD_DIM)

    def one_frame(pair):
        frame_hidden, frame_norm = pair
        queries = jnp.dot(frame_norm, w_query, preferred_element_type=jnp.float32).astype(
            jnp.bfloat16
        )
        query_heads = queries.reshape(pixels, heads, HEAD_DIM)
        scores = (
            jnp.einsum("qhd,rhd->qhr", query_heads, key_heads, preferred_element_type=jnp.float32)
            * 0.125
        )
        peak = jnp.max(scores, -1, keepdims=True)
        weights = jnp.exp(scores - peak)
        total = jnp.sum(weights, -1)
        summed = jnp.einsum(
            "qhr,rhd->qhd",
            weights.astype(jnp.bfloat16),
            value_heads,
            preferred_element_type=jnp.float32,
        )
        attended = (summed / total[..., None]).reshape(pixels, width).astype(jnp.bfloat16)
        mixed = frame_hidden.astype(jnp.float32) + jnp.dot(
            attended, w_out, preferred_element_type=jnp.float32
        )
        return mixed.astype(jnp.bfloat16)

    return lax.map(one_frame, (hidden, norm2))


def solution(mesh):
    return jax.shard_map(
        shards,
        mesh=mesh,
        in_specs=(
            P(("clip", "group"), None, None),
            P(),
            P(("clip", "group")),
            P(),
            P(),
            P(),
            P(),
            P(),
            P(),
            P(),
            P(),
        ),
        out_specs=P(("clip", "group"), None, None),
        check_vma=False,
    )
```

```python
import math

import jax
import jax.numpy as jnp
import numpy as np
from jax import lax
from jax.experimental import pallas as pl
from jax.experimental.pallas import tpu as pltpu
from jax.sharding import PartitionSpec as P

HEAD_DIM = 64
PH = 32
PW = 20
PIX = PH * PW
C = 640
PAIRS = C // (2 * HEAD_DIM)
ROWS = 1024
CHUNK = 256
AXES = ("clip", "group")
VMEM = 56 * 2**20
SCALE = math.log2(math.e) / math.sqrt(HEAD_DIM)
LOW, HIGH = 2.0**-100, 2.0**110


def place(device):
    clip, group = divmod(device, 32)
    x_low, y = divmod(clip, 4)
    x_high, rest = divmod(group, 16)
    z, core = divmod(rest, 2)
    return x_high * 2 + x_low, y, z, core


def groups_by(key):
    found = {}
    for device in range(256):
        found.setdefault(key(*place(device)), []).append(device)
    return list(found.values())


def exchange(copies, groups):
    return lax.all_to_all(copies, AXES, 0, 0, axis_index_groups=groups, tiled=False)


def dot(a, b):
    return jnp.dot(a, b, preferred_element_type=jnp.float32)


def normalize(values, gain):
    return values * lax.rsqrt(jnp.mean(values * values, -1, keepdims=True) + 1e-06) * gain


def time_bias(timestep, w_time):
    half = w_time.shape[0] // 2
    freqs = jnp.exp(-math.log(10000.0) * jnp.arange(half, dtype=jnp.float32) / half)
    angle = timestep.astype(jnp.float32)[0] * freqs
    embed = jnp.concatenate([jnp.cos(angle), jnp.sin(angle)])
    return jnp.dot(
        jax.nn.silu(embed)[None, :],
        w_time,
        precision=lax.Precision.HIGHEST,
        preferred_element_type=jnp.float32,
    )


def whole(shape, **kwargs):
    return pl.BlockSpec(shape, lambda *_: (0,) * len(shape), **kwargs)


def call(kernel, name, out_shape, in_specs, out_specs, flops, moved, **kwargs):
    if in_specs is not None:
        kwargs.update(in_specs=in_specs, out_specs=out_specs)
    return pl.pallas_call(
        kernel,
        out_shape=out_shape,
        name=name,
        compiler_params=pltpu.CompilerParams(vmem_limit_bytes=VMEM),
        cost_estimate=pl.CostEstimate(flops=flops, bytes_accessed=moved, transcendentals=0),
        **kwargs,
    )


def own_taps(latents_ref, gain_ref, taps_ref, temb_ref, acc_ref):
    gain = gain_ref[...]
    source = [latents_ref[f].astype(jnp.float32) for f in range(2)]
    norm = [normalize(s, gain).astype(jnp.bfloat16) for s in source]
    temb = temb_ref[...]
    acc_ref[0] = source[0] + temb + dot(norm[0], taps_ref[1]) + dot(norm[1], taps_ref[2])
    acc_ref[1] = source[1] + temb + dot(norm[0], taps_ref[0]) + dot(norm[1], taps_ref[1])


def finish(halo_ref, acc, tap, gain_pre, gain_mid):
    norm = normalize(halo_ref[0].astype(jnp.float32), gain_pre).astype(jnp.bfloat16)
    hidden = (acc + dot(norm, tap)).astype(jnp.bfloat16)
    return hidden, normalize(hidden.astype(jnp.float32), gain_mid).astype(jnp.bfloat16)


def chosen_frame(
    pick_ref, before_ref, after_ref, acc_ref, taps_ref, gain_pre_ref, gain_mid_ref, region_ref,
    hidden_ref, norm_ref, ctx_ref,
):
    def run(halo_ref, frame, tap):
        hidden, norm = finish(
            halo_ref, acc_ref[frame], taps_ref[tap], gain_pre_ref[...], gain_mid_ref[...]
        )
        hidden_ref[...] = hidden
        norm_ref[...] = norm
        pooled = dot(region_ref[...], norm) * (4.0 / PIX)
        rows = normalize(pooled, 1.0).astype(jnp.bfloat16)[:4]
        for copy in range(ctx_ref.shape[0]):
            ctx_ref[copy] = rows

    pl.when(pick_ref[0] == 0)(lambda: run(before_ref, 0, 0))
    pl.when(pick_ref[0] != 0)(lambda: run(after_ref, 1, 2))


def other_frame(
    pick_ref, before_ref, after_ref, acc_ref, taps_ref, gain_pre_ref, gain_mid_ref, w_query_ref,
    hidden_in_ref, norm_in_ref, hidden_ref, query_ref,
):
    def queries(norm):
        return (dot(norm, w_query_ref[...]) * SCALE).astype(jnp.bfloat16)

    def run(halo_ref, frame, tap):
        hidden, norm = finish(
            halo_ref, acc_ref[frame], taps_ref[tap], gain_pre_ref[...], gain_mid_ref[...]
        )
        hidden_ref[1] = hidden
        query_ref[1] = queries(norm)

    pl.when(pick_ref[0] == 0)(lambda: run(after_ref, 1, 2))
    pl.when(pick_ref[0] != 0)(lambda: run(before_ref, 0, 0))
    hidden_ref[0] = hidden_in_ref[...]
    query_ref[0] = queries(norm_in_ref[...])


def attention(
    pick_ref, ctx_ref, w_key_ref, w_value_ref, w_out_ref, query_ref, hidden_ref, out_ref,
    key_ref, value_ref, mixed_ref,
):
    @pl.when(pl.program_id(0) == 0)
    def _():
        left = lax.broadcasted_iota(jnp.int32, (ROWS, 128), 1) < HEAD_DIM
        zero = jnp.zeros((HEAD_DIM, ROWS), jnp.bfloat16)
        for pair in range(PAIRS):
            lanes = slice(128 * pair, 128 * pair + 128)
            keys = dot(ctx_ref[...], w_key_ref[:, lanes]).T.astype(jnp.bfloat16)
            key_ref[2 * pair, :HEAD_DIM] = keys[:HEAD_DIM]
            key_ref[2 * pair, HEAD_DIM:] = zero
            key_ref[2 * pair + 1, :HEAD_DIM] = zero
            key_ref[2 * pair + 1, HEAD_DIM:] = keys[HEAD_DIM:]
            values = dot(ctx_ref[...], w_value_ref[:, lanes])
            value_ref[2 * pair, :, :128] = jnp.where(left, values, 0.0).astype(jnp.bfloat16)
            value_ref[2 * pair, :, 128:] = jnp.where(left, 1.0, 0.0).astype(jnp.bfloat16)
            value_ref[2 * pair + 1, :, :128] = jnp.where(left, 0.0, values).astype(jnp.bfloat16)
            value_ref[2 * pair + 1, :, 128:] = jnp.where(left, 0.0, 1.0).astype(jnp.bfloat16)

    inside = None
    for pair in range(PAIRS):
        lanes = slice(128 * pair, 128 * pair + 128)
        query = query_ref[0, :, lanes]
        total = None
        for side in range(2):
            for start in range(0, ROWS, CHUNK):
                rows = slice(start, start + CHUNK)
                weights = jnp.exp2(dot(query, key_ref[2 * pair + side, :, rows]))
                part = dot(weights.astype(jnp.bfloat16), value_ref[2 * pair + side, rows])
                total = part if total is None else total + part
        sums = total[:, 128:]
        good = jnp.where((sums >= LOW) & (sums <= HIGH), 1.0, 0.0)
        inside = good if inside is None else jnp.minimum(inside, good)
        mixed_ref[:, lanes] = (total[:, :128] / sums).astype(jnp.bfloat16)

    @pl.when(jnp.min(inside) < 0.5)
    def _():
        def some_rows(step, carry):
            rows = pl.ds(pl.multiple_of(step * 128, 128), 128)
            for pair in range(PAIRS):
                lanes = slice(128 * pair, 128 * pair + 128)
                query = query_ref[0, rows, lanes]
                total = jnp.zeros((128, 256), jnp.float32)
                for side in range(2):
                    scores = dot(query, key_ref[2 * pair + side])
                    weights = jnp.exp2(scores - jnp.max(scores, -1, keepdims=True))
                    total += dot(weights.astype(jnp.bfloat16), value_ref[2 * pair + side])
                mixed_ref[rows, lanes] = (total[:, :128] / total[:, 128:]).astype(jnp.bfloat16)
            return carry

        lax.fori_loop(0, PIX // 128, some_rows, 0)

    projected = dot(mixed_ref[...], w_out_ref[...])
    out_ref[0] = (hidden_ref[0].astype(jnp.float32) + projected).astype(jnp.bfloat16)


def shards(
    latents,
    timestep,
    context_frame,
    gain_pre,
    w_temporal,
    w_time,
    gain_mid,
    w_query,
    w_key,
    w_value,
    w_out,
):
    up = [(i, (i + 1) % 256) for i in range(256)]
    down = [(j, i) for i, j in up]
    before = lax.ppermute(latents[1:], AXES, up)
    after = lax.ppermute(latents[:1], AXES, down)

    gain_pre = gain_pre.reshape(1, C)
    gain_mid = gain_mid.reshape(1, C)
    frame, pair = (PIX, C), (2, PIX, C)
    half, single = jnp.bfloat16, jnp.float32
    mac = 2 * PIX * C * C
    temb = time_bias(timestep, w_time)
    acc = call(
        own_taps,
        "own_taps",
        jax.ShapeDtypeStruct(pair, single),
        [whole(pair), whole((1, C)), whole((3, C, C)), whole((1, C))],
        whole(pair),
        4 * mac,
        8 * 10**6,
    )(latents, gain_pre, w_temporal, temb)

    region = np.zeros((16, PIX), np.float32)
    pixel = np.arange(PIX)
    region[(pixel // PW) // (PH // 2) * 2 + (pixel % PW) // (PW // 2), pixel] = 1.0
    scalar = pl.BlockSpec(memory_space=pltpu.SMEM)
    shared = [
        scalar,
        whole((1,) + frame),
        whole((1,) + frame),
        whole(pair),
        whole((3, C, C)),
        whole((1, C)),
        whole((1, C)),
    ]
    hidden, norm, ctx = call(
        chosen_frame,
        "chosen_frame",
        (
            jax.ShapeDtypeStruct(frame, half),
            jax.ShapeDtypeStruct(frame, half),
            jax.ShapeDtypeStruct((8, 4, C), half),
        ),
        shared + [whole((16, PIX))],
        (whole(frame), whole(frame), whole((8, 4, C))),
        mac,
        8 * 10**6,
    )(context_frame, before, after, acc, w_temporal, gain_pre, gain_mid, jnp.asarray(region, half))

    line = exchange(ctx, groups_by(lambda x, y, z, core: (x, y, core))).reshape(32, C)
    plane = exchange(
        jnp.broadcast_to(line[None], (16, 32, C)), groups_by(lambda x, y, z, core: (z, core))
    ).reshape(512, C)
    swapped = lax.ppermute(plane, AXES, [(i, i ^ 1) for i in range(256)])

    hidden, query = call(
        other_frame,
        "other_frame",
        (jax.ShapeDtypeStruct(pair, half), jax.ShapeDtypeStruct(pair, half)),
        shared + [whole((C, C)), whole(frame), whole(frame)],
        (whole(pair), whole(pair)),
        3 * mac,
        12 * 10**6,
    )(context_frame, before, after, acc, w_temporal, gain_pre, gain_mid, w_query, hidden, norm)

    by_frame = pl.BlockSpec((1,) + frame, lambda i, *_: (i, 0, 0))
    return call(
        attention,
        "attention",
        jax.ShapeDtypeStruct(pair, half),
        None,
        None,
        2 * 10**10,
        10 * 10**6,
        grid_spec=pltpu.PrefetchScalarGridSpec(
            num_scalar_prefetch=1,
            grid=(2,),
            in_specs=[whole((ROWS, C))] + [whole((C, C))] * 3 + [by_frame] * 2,
            out_specs=pl.BlockSpec((1,) + frame, lambda i, pick: (jnp.where(pick[0] == 0, i, 1 - i), 0, 0)),
            scratch_shapes=[
                pltpu.VMEM((2 * PAIRS, 128, ROWS), half),
                pltpu.VMEM((2 * PAIRS, ROWS, 256), half),
                pltpu.VMEM(frame, half),
            ],
        ),
    )(context_frame, jnp.concatenate([plane, swapped]), w_key, w_value, w_out, query, hidden)


def solution(mesh):
    return jax.shard_map(
        shards,
        mesh=mesh,
        in_specs=(
            P(("clip", "group"), None, None),
            P(),
            P(("clip", "group")),
            P(),
            P(),
            P(),
            P(),
            P(),
            P(),
            P(),
            P(),
        ),
        out_specs=P(("clip", "group"), None, None),
        check_vma=False,
    )
```

```python
import math

import jax
import jax.numpy as jnp
import numpy as np
from jax import lax
from jax.experimental import pallas as pl
from jax.experimental.pallas import tpu as pltpu
from jax.sharding import PartitionSpec as P

HEAD_DIM = 64
PH = 32
PW = 20
PIX = PH * PW
C = 640
PAIRS = C // (2 * HEAD_DIM)
ROWS = 1024
CHUNK = 256
STRIP = 128
AXES = ("clip", "group")
VMEM = 60 * 2**20
TAPS_VMEM = 56 * 2**20
SCALE = math.log2(math.e) / math.sqrt(HEAD_DIM)
LOW, HIGH = 2.0**-100, 2.0**110


def place(device):
    clip, group = divmod(device, 32)
    x_low, y = divmod(clip, 4)
    x_high, rest = divmod(group, 16)
    z, core = divmod(rest, 2)
    return x_high * 2 + x_low, y, z, core


def groups_by(key):
    found = {}
    for device in range(256):
        found.setdefault(key(*place(device)), []).append(device)
    return list(found.values())


def exchange(copies, groups):
    return lax.all_to_all(copies, AXES, 0, 0, axis_index_groups=groups, tiled=False)


def dot(a, b):
    return jnp.dot(a, b, preferred_element_type=jnp.float32)


def normalize(values, gain):
    return values * lax.rsqrt(jnp.mean(values * values, -1, keepdims=True) + 1e-06) * gain


def time_bias(timestep, w_time):
    half = w_time.shape[0] // 2
    freqs = jnp.exp(-math.log(10000.0) * jnp.arange(half, dtype=jnp.float32) / half)
    angle = timestep.astype(jnp.float32)[0] * freqs
    embed = jnp.concatenate([jnp.cos(angle), jnp.sin(angle)])
    return jnp.dot(
        jax.nn.silu(embed)[None, :],
        w_time,
        precision=lax.Precision.HIGHEST,
        preferred_element_type=jnp.float32,
    )


def whole(shape, **kwargs):
    return pl.BlockSpec(shape, lambda *_: (0,) * len(shape), **kwargs)


def call(kernel, name, out_shape, in_specs, out_specs, flops, moved, vmem=VMEM, **kwargs):
    if in_specs is not None:
        kwargs.update(in_specs=in_specs, out_specs=out_specs)
    return pl.pallas_call(
        kernel,
        out_shape=out_shape,
        name=name,
        compiler_params=pltpu.CompilerParams(vmem_limit_bytes=vmem),
        cost_estimate=pl.CostEstimate(flops=flops, bytes_accessed=moved, transcendentals=0),
        **kwargs,
    )


def copy_all(pairs, sems):
    copies = [pltpu.make_async_copy(a, b, sems.at[i]) for i, (a, b) in enumerate(pairs)]
    for copy in copies:
        copy.start()
    return copies


def strips():
    return [slice(start, start + STRIP) for start in range(0, PIX, STRIP)]


def own_taps(latents_ref, gain_ref, temb_ref, taps_ref, acc_ref, big_ref, part_ref, sems, out_sems):
    order = ((1, 0), (2, 1))
    places = [
        (taps_ref.at[order[i][j]], big_ref.at[pl.ds(C * i, C), pl.ds(C * j, C)])
        for i in range(2)
        for j in range(2)
    ]
    copies = copy_all(places, sems)
    gain, temb = gain_ref[...], temb_ref[...]
    writes = []
    for number, rows in enumerate(strips()):
        source = [latents_ref[f, rows].astype(jnp.float32) for f in range(2)]
        norm = jnp.concatenate([normalize(s, gain).astype(jnp.bfloat16) for s in source], axis=1)
        if number == 0:
            for copy in copies:
                copy.wait()
        both = dot(norm, big_ref[...])
        for f in range(2):
            part_ref[f, rows] = source[f] + temb + both[:, C * f : C * f + C]
            copy = pltpu.make_async_copy(
                part_ref.at[f, rows], acc_ref.at[f, rows], out_sems.at[2 * number + f]
            )
            copy.start()
            writes.append(copy)
    for copy in writes:
        copy.wait()


def chosen_frame(
    pick_ref, before_ref, after_ref, gain_pre_ref, gain_mid_ref, region_ref, acc_ref, taps_ref,
    hidden_out, ctx_ref, hidden_ref, part_ref, tap_ref, sems, out_sems,
):
    first = pick_ref[0] == 0
    frame = jnp.where(first, 0, 1)
    tap_copy, part_copy = copy_all(
        [(taps_ref.at[2 * frame], tap_ref), (acc_ref.at[frame], part_ref)], sems
    )
    gain_pre, gain_mid = gain_pre_ref[...], gain_mid_ref[...]
    pooled = None
    writes = []
    for number, rows in enumerate(strips()):
        halo = jnp.where(first, before_ref[0, rows], after_ref[0, rows]).astype(jnp.float32)
        norm = normalize(halo, gain_pre).astype(jnp.bfloat16)
        if number == 0:
            tap_copy.wait()
            part_copy.wait()
        hidden = (part_ref[rows] + dot(norm, tap_ref[...])).astype(jnp.bfloat16)
        hidden_ref[rows] = hidden
        writes += copy_all([(hidden_ref.at[rows], hidden_out.at[rows])], out_sems.at[pl.ds(number, 1)])
        norm = normalize(hidden.astype(jnp.float32), gain_mid).astype(jnp.bfloat16)
        sums = dot(region_ref[:, rows], norm)
        pooled = sums if pooled is None else pooled + sums
    rows = normalize(pooled * (4.0 / PIX), 1.0).astype(jnp.bfloat16)[:4]
    for copy in range(ctx_ref.shape[0]):
        ctx_ref[copy] = rows
    for copy in writes:
        copy.wait()


def other_frame(
    pick_ref, before_ref, after_ref, gain_pre_ref, gain_mid_ref, chosen_hbm, acc_ref, taps_ref,
    w_query_hbm, hidden_out, query_out, hidden_ref, query_ref, part_ref, tap_ref, chosen_ref,
    w_query_ref, sems, out_sems,
):
    first = pick_ref[0] == 0
    frame = jnp.where(first, 1, 0)
    copies = copy_all(
        [
            (chosen_hbm, chosen_ref),
            (w_query_hbm, w_query_ref),
            (taps_ref.at[2 * frame], tap_ref),
            (acc_ref.at[frame], part_ref),
        ],
        sems,
    )
    gain_pre, gain_mid = gain_pre_ref[...], gain_mid_ref[...]
    for copy in copies[:2]:
        copy.wait()

    def queries(slot, rows, hidden):
        norm = normalize(hidden.astype(jnp.float32), gain_mid).astype(jnp.bfloat16)
        query_ref[slot, rows] = (dot(norm, w_query_ref[...]) * SCALE).astype(jnp.bfloat16)

    for rows in strips():
        queries(0, rows, chosen_ref[rows])
    writes = copy_all([(query_ref.at[0], query_out.at[0])], out_sems.at[pl.ds(0, 1)])
    for copy in copies[2:]:
        copy.wait()
    for rows in strips():
        halo = jnp.where(first, after_ref[0, rows], before_ref[0, rows]).astype(jnp.float32)
        norm = normalize(halo, gain_pre).astype(jnp.bfloat16)
        hidden = (part_ref[rows] + dot(norm, tap_ref[...])).astype(jnp.bfloat16)
        hidden_ref[rows] = hidden
        queries(1, rows, hidden)
    writes += copy_all(
        [(query_ref.at[1], query_out.at[1]), (hidden_ref, hidden_out)], out_sems.at[pl.ds(1, 2)]
    )
    for copy in writes:
        copy.wait()


def attention(
    pick_ref, near_ref, far_ref, w_key_hbm, w_value_hbm, w_out_hbm, query_hbm, chosen_hbm, other_hbm,
    out_ref, key_ref, value_ref, mixed_ref, w_key_ref, w_value_ref, w_out_ref, query_ref, hidden_ref,
    sems,
):
    step = pl.program_id(0)
    moves = [
        pltpu.make_async_copy(a, b, sems.at[i])
        for i, (a, b) in enumerate(
            [
                (w_key_hbm, w_key_ref),
                (w_value_hbm, w_value_ref),
                (query_hbm, query_ref),
                (w_out_hbm, w_out_ref),
                (chosen_hbm, hidden_ref.at[0]),
                (other_hbm, hidden_ref.at[1]),
            ]
        )
    ]

    @pl.when(step == 0)
    def _():
        for move in moves:
            move.start()
        half = ROWS // 2
        left = lax.broadcasted_iota(jnp.int32, (half, 128), 1) < HEAD_DIM
        zero = jnp.zeros((HEAD_DIM, half), jnp.bfloat16)
        moves[0].wait()
        for number, ctx_ref in enumerate((near_ref, far_ref)):
            rows = slice(half * number, half * number + half)
            for pair in range(PAIRS):
                lanes = slice(128 * pair, 128 * pair + 128)
                keys = dot(ctx_ref[...], w_key_ref[:, lanes]).T.astype(jnp.bfloat16)
                key_ref[2 * pair, :HEAD_DIM, rows] = keys[:HEAD_DIM]
                key_ref[2 * pair, HEAD_DIM:, rows] = zero
                key_ref[2 * pair + 1, :HEAD_DIM, rows] = zero
                key_ref[2 * pair + 1, HEAD_DIM:, rows] = keys[HEAD_DIM:]
        moves[1].wait()
        for number, ctx_ref in enumerate((near_ref, far_ref)):
            rows = slice(half * number, half * number + half)
            for pair in range(PAIRS):
                lanes = slice(128 * pair, 128 * pair + 128)
                values = dot(ctx_ref[...], w_value_ref[:, lanes])
                for side in range(2):
                    mine = left if side == 0 else ~left
                    value_ref[2 * pair + side, rows, :128] = jnp.where(mine, values, 0.0).astype(
                        jnp.bfloat16
                    )
                    value_ref[2 * pair + side, rows, 128:] = jnp.where(mine, 1.0, 0.0).astype(
                        jnp.bfloat16
                    )
        for move in moves[2:]:
            move.wait()

    inside = None
    for pair in range(PAIRS):
        lanes = slice(128 * pair, 128 * pair + 128)
        query = query_ref[step, :, lanes]
        total = None
        for side in range(2):
            for start in range(0, ROWS, CHUNK):
                rows = slice(start, start + CHUNK)
                weights = jnp.exp2(dot(query, key_ref[2 * pair + side, :, rows]))
                part = dot(weights.astype(jnp.bfloat16), value_ref[2 * pair + side, rows])
                total = part if total is None else total + part
        sums = total[:, 128:]
        good = jnp.where((sums >= LOW) & (sums <= HIGH), 1.0, 0.0)
        inside = good if inside is None else jnp.minimum(inside, good)
        mixed_ref[:, lanes] = (total[:, :128] / sums).astype(jnp.bfloat16)

    @pl.when(jnp.min(inside) < 0.5)
    def _():
        def some_rows(strip, carry):
            rows = pl.ds(pl.multiple_of(strip * 128, 128), 128)
            for pair in range(PAIRS):
                lanes = slice(128 * pair, 128 * pair + 128)
                query = query_ref[step, rows, lanes]
                total = jnp.zeros((128, 256), jnp.float32)
                for side in range(2):
                    scores = dot(query, key_ref[2 * pair + side])
                    weights = jnp.exp2(scores - jnp.max(scores, -1, keepdims=True))
                    total += dot(weights.astype(jnp.bfloat16), value_ref[2 * pair + side])
                mixed_ref[rows, lanes] = (total[:, :128] / total[:, 128:]).astype(jnp.bfloat16)
            return carry

        lax.fori_loop(0, PIX // 128, some_rows, 0)

    projected = dot(mixed_ref[...], w_out_ref[...])
    out_ref[0] = (hidden_ref[step].astype(jnp.float32) + projected).astype(jnp.bfloat16)


def shards(
    latents,
    timestep,
    context_frame,
    gain_pre,
    w_temporal,
    w_time,
    gain_mid,
    w_query,
    w_key,
    w_value,
    w_out,
):
    up = [(i, (i + 1) % 256) for i in range(256)]
    down = [(j, i) for i, j in up]
    after = lax.ppermute(latents[:1], AXES, down)
    before = lax.ppermute(latents[1:], AXES, up)

    gain_pre = gain_pre.reshape(1, C)
    gain_mid = gain_mid.reshape(1, C)
    frame, pair, square = (PIX, C), (2, PIX, C), (C, C)
    half, single = jnp.bfloat16, jnp.float32
    mac = 2 * PIX * C * C
    here, there = pl.BlockSpec(memory_space=pltpu.VMEM), pl.BlockSpec(memory_space=pltpu.HBM)
    scalar = pl.BlockSpec(memory_space=pltpu.SMEM)
    temb = time_bias(timestep, w_time)
    acc = call(
        own_taps,
        "own_taps",
        jax.ShapeDtypeStruct(pair, single),
        [here, here, here, there],
        there,
        4 * mac,
        8 * 10**6,
        TAPS_VMEM,
        scratch_shapes=[
            pltpu.VMEM((2 * C, 2 * C), half),
            pltpu.VMEM(pair, single),
            pltpu.SemaphoreType.DMA((4,)),
            pltpu.SemaphoreType.DMA((2 * PIX // STRIP,)),
        ],
    )(latents, gain_pre, temb, w_temporal)

    region = np.zeros((16, PIX), np.float32)
    pixel = np.arange(PIX)
    region[(pixel // PW) // (PH // 2) * 2 + (pixel % PW) // (PW // 2), pixel] = 1.0
    chosen, ctx = call(
        chosen_frame,
        "chosen_frame",
        (jax.ShapeDtypeStruct(frame, half), jax.ShapeDtypeStruct((8, 4, C), half)),
        [scalar, here, here, here, here, here, there, there],
        (there, here),
        mac,
        8 * 10**6,
        scratch_shapes=[
            pltpu.VMEM(frame, half),
            pltpu.VMEM(frame, single),
            pltpu.VMEM(square, half),
            pltpu.SemaphoreType.DMA((2,)),
            pltpu.SemaphoreType.DMA((PIX // STRIP,)),
        ],
    )(context_frame, before, after, gain_pre, gain_mid, jnp.asarray(region, half), acc, w_temporal)

    line = exchange(ctx, groups_by(lambda x, y, z, core: (x, y, core))).reshape(32, C)
    other, query = call(
        other_frame,
        "other_frame",
        (jax.ShapeDtypeStruct(frame, half), jax.ShapeDtypeStruct(pair, half)),
        [scalar, here, here, here, here, there, there, there, there],
        (there, there),
        3 * mac,
        12 * 10**6,
        scratch_shapes=[
            pltpu.VMEM(frame, half),
            pltpu.VMEM(pair, half),
            pltpu.VMEM(frame, single),
            pltpu.VMEM(square, half),
            pltpu.VMEM(frame, half),
            pltpu.VMEM(square, half),
            pltpu.SemaphoreType.DMA((4,)),
            pltpu.SemaphoreType.DMA((3,)),
        ],
    )(context_frame, before, after, gain_pre, gain_mid, chosen, acc, w_temporal, w_query)

    line, other, query = lax.optimization_barrier((line, other, query))
    plane = exchange(
        jnp.broadcast_to(line[None], (16, 32, C)), groups_by(lambda x, y, z, core: (z, core))
    ).reshape(512, C)
    swapped = lax.ppermute(plane, AXES, [(i, i ^ 1) for i in range(256)])

    return call(
        attention,
        "attention",
        jax.ShapeDtypeStruct(pair, half),
        None,
        None,
        2 * 10**10,
        10 * 10**6,
        grid_spec=pltpu.PrefetchScalarGridSpec(
            num_scalar_prefetch=1,
            grid=(2,),
            in_specs=[whole((ROWS // 2, C))] * 2 + [there] * 6,
            out_specs=pl.BlockSpec(
                (1,) + frame, lambda i, pick: (jnp.where(pick[0] == 0, i, 1 - i), 0, 0)
            ),
            scratch_shapes=[
                pltpu.VMEM((2 * PAIRS, 128, ROWS), half),
                pltpu.VMEM((2 * PAIRS, ROWS, 256), half),
                pltpu.VMEM(frame, half),
                pltpu.VMEM(square, half),
                pltpu.VMEM(square, half),
                pltpu.VMEM(square, half),
                pltpu.VMEM(pair, half),
                pltpu.VMEM(pair, half),
                pltpu.SemaphoreType.DMA((6,)),
            ],
        ),
    )(context_frame, plane, swapped, w_key, w_value, w_out, query, chosen, other)


def solution(mesh):
    return jax.shard_map(
        shards,
        mesh=mesh,
        in_specs=(
            P(("clip", "group"), None, None),
            P(),
            P(("clip", "group")),
            P(),
            P(),
            P(),
            P(),
            P(),
            P(),
            P(),
            P(),
        ),
        out_specs=P(("clip", "group"), None, None),
        check_vma=False,
    )
```

```python
import math

import jax
import jax.numpy as jnp
import numpy as np
from jax import lax
from jax.experimental import pallas as pl
from jax.experimental.pallas import tpu as pltpu
from jax.sharding import PartitionSpec as P

HEAD_DIM = 64
PH = 32
PW = 20
PIX = PH * PW
C = 640
PAIRS = C // (2 * HEAD_DIM)
ROWS = 1024
CHUNK = 256
STRIP = 320
AXES = ("clip", "group")
MIB = 2**20
TAPS_VMEM = 24 * MIB
CONTEXT_VMEM = 24 * MIB
HIDDEN_VMEM = 56 * MIB
ATTENTION_VMEM = 52 * MIB
SCALE = math.log2(math.e) / math.sqrt(HEAD_DIM)
LOW, HIGH = 2.0**-100, 2.0**110


def place(device):
    clip, group = divmod(device, 32)
    x_low, y = divmod(clip, 4)
    x_high, rest = divmod(group, 16)
    z, core = divmod(rest, 2)
    return x_high * 2 + x_low, y, z, core


def groups_by(key):
    found = {}
    for device in range(256):
        found.setdefault(key(*place(device)), []).append(device)
    return list(found.values())


def exchange(copies, groups):
    return lax.all_to_all(copies, AXES, 0, 0, axis_index_groups=groups, tiled=False)


def dot(a, b):
    return jnp.dot(a, b, preferred_element_type=jnp.float32)


def normalize(values, gain):
    return values * lax.rsqrt(jnp.mean(values * values, -1, keepdims=True) + 1e-06) * gain


def time_bias(timestep, w_time):
    half = w_time.shape[0] // 2
    freqs = jnp.exp(-math.log(10000.0) * jnp.arange(half, dtype=jnp.float32) / half)
    angle = timestep.astype(jnp.float32)[0] * freqs
    embed = jnp.concatenate([jnp.cos(angle), jnp.sin(angle)])
    return jnp.dot(
        jax.nn.silu(embed)[None, :],
        w_time,
        precision=lax.Precision.HIGHEST,
        preferred_element_type=jnp.float32,
    )


def whole(shape, **kwargs):
    return pl.BlockSpec(shape, lambda *_: (0,) * len(shape), **kwargs)


def call(kernel, name, out_shape, in_specs, out_specs, flops, moved, vmem, **kwargs):
    if in_specs is not None:
        kwargs.update(in_specs=in_specs, out_specs=out_specs)
    return pl.pallas_call(
        kernel,
        out_shape=out_shape,
        name=name,
        compiler_params=pltpu.CompilerParams(vmem_limit_bytes=vmem),
        cost_estimate=pl.CostEstimate(flops=flops, bytes_accessed=moved, transcendentals=0),
        **kwargs,
    )


def copy_all(pairs, sems):
    copies = [pltpu.make_async_copy(a, b, sems.at[i]) for i, (a, b) in enumerate(pairs)]
    for copy in copies:
        copy.start()
    return copies


def strips():
    return [slice(start, start + STRIP) for start in range(0, PIX, STRIP)]


def own_taps(
    pick_ref, latents_ref, gain_ref, temb_ref, taps_ref, chosen_ref, other_ref, big_ref, sems
):
    first = pick_ref[0] == 0
    order = ((1, 0), (2, 1))
    copies = copy_all(
        [
            (taps_ref.at[order[i][j]], big_ref.at[pl.ds(C * i, C), pl.ds(C * j, C)])
            for i in range(2)
            for j in range(2)
        ],
        sems,
    )
    gain, temb = gain_ref[...], temb_ref[...]
    for copy in copies:
        copy.wait()
    for rows in strips():
        source = [latents_ref[f, rows].astype(jnp.float32) for f in range(2)]
        norm = jnp.concatenate([normalize(s, gain).astype(jnp.bfloat16) for s in source], axis=1)
        both = dot(norm, big_ref[...])
        parts = [source[f] + temb + both[:, C * f : C * f + C] for f in range(2)]
        chosen_ref[rows] = jnp.where(first, parts[0], parts[1])
        other_ref[rows] = jnp.where(first, parts[1], parts[0])


def context_rows(
    pick_ref, before_ref, after_ref, gain_pre_ref, gain_mid_ref, side_ref, part_ref, taps_ref, ctx_ref
):
    first = pick_ref[0] == 0
    tap = jnp.where(first, 0, 2)
    gain_pre, gain_mid = gain_pre_ref[...], gain_mid_ref[...]
    tile = side_ref.shape[0]
    sums = []
    for half in range(2):
        rows = slice(half * PIX // 2, (half + 1) * PIX // 2)
        halo = jnp.where(first, before_ref[0, rows], after_ref[0, rows]).astype(jnp.float32)
        norm = normalize(halo, gain_pre).astype(jnp.bfloat16)
        hidden = (part_ref[rows] + dot(norm, taps_ref[tap])).astype(jnp.bfloat16)
        norm = normalize(hidden.astype(jnp.float32), gain_mid).astype(jnp.bfloat16)
        norm = norm.astype(jnp.float32).reshape(PIX // 2 // tile, tile, C)
        for side in range(2):
            here = jnp.sum(norm * side_ref[:, C * side : C * side + C], axis=0)
            sums.append(jnp.sum(here, axis=0, keepdims=True))
    pooled = jnp.concatenate(sums, axis=0) * (4.0 / PIX)
    rows = normalize(pooled, 1.0).astype(jnp.bfloat16)
    for copy in range(ctx_ref.shape[0]):
        ctx_ref[copy] = rows


def hidden_queries(
    pick_ref, before_ref, after_ref, gain_pre_ref, gain_mid_ref, part_hbm, other_part_hbm, taps_hbm,
    w_query_hbm, hidden_ref, query_ref, part_ref, taps_ref, w_query_ref, sems,
):
    first = pick_ref[0] == 0
    copies = copy_all(
        [
            (taps_hbm.at[0], taps_ref.at[0]),
            (taps_hbm.at[2], taps_ref.at[1]),
            (part_hbm, part_ref.at[0]),
            (other_part_hbm, part_ref.at[1]),
            (w_query_hbm, w_query_ref),
        ],
        sems,
    )
    gain_pre, gain_mid = gain_pre_ref[...], gain_mid_ref[...]
    for copy in copies:
        copy.wait()
    for slot in range(2):
        tap = jnp.where(first, slot, 1 - slot)
        for rows in strips():
            halo = jnp.where(tap == 0, before_ref[0, rows], after_ref[0, rows]).astype(jnp.float32)
            norm = normalize(halo, gain_pre).astype(jnp.bfloat16)
            hidden = (part_ref[slot, rows] + dot(norm, taps_ref[tap])).astype(jnp.bfloat16)
            hidden_ref[slot, rows] = hidden
            norm = normalize(hidden.astype(jnp.float32), gain_mid).astype(jnp.bfloat16)
            query_ref[slot, rows] = (dot(norm, w_query_ref[...]) * SCALE).astype(jnp.bfloat16)


def attention(
    pick_ref, near_ref, far_ref, w_key_hbm, w_value_hbm, w_out_hbm, query_hbm, hidden_hbm,
    out_ref, key_ref, value_ref, mixed_ref, w_key_ref, w_value_ref, w_out_ref, query_ref, hidden_ref,
    sems,
):
    step = pl.program_id(0)
    moves = [
        pltpu.make_async_copy(a, b, sems.at[i])
        for i, (a, b) in enumerate(
            [
                (w_key_hbm, w_key_ref),
                (w_value_hbm, w_value_ref),
                (query_hbm, query_ref),
                (w_out_hbm, w_out_ref),
                (hidden_hbm, hidden_ref),
            ]
        )
    ]

    @pl.when(step == 0)
    def _():
        for move in moves:
            move.start()
        half = ROWS // 2
        left = lax.broadcasted_iota(jnp.int32, (half, 128), 1) < HEAD_DIM
        zero = jnp.zeros((HEAD_DIM, half), jnp.bfloat16)
        moves[0].wait()
        for number, ctx_ref in enumerate((near_ref, far_ref)):
            rows = slice(half * number, half * number + half)
            for pair in range(PAIRS):
                lanes = slice(128 * pair, 128 * pair + 128)
                keys = dot(ctx_ref[...], w_key_ref[:, lanes]).T.astype(jnp.bfloat16)
                key_ref[2 * pair, :HEAD_DIM, rows] = keys[:HEAD_DIM]
                key_ref[2 * pair, HEAD_DIM:, rows] = zero
                key_ref[2 * pair + 1, :HEAD_DIM, rows] = zero
                key_ref[2 * pair + 1, HEAD_DIM:, rows] = keys[HEAD_DIM:]
        moves[1].wait()
        for number, ctx_ref in enumerate((near_ref, far_ref)):
            rows = slice(half * number, half * number + half)
            for pair in range(PAIRS):
                lanes = slice(128 * pair, 128 * pair + 128)
                values = dot(ctx_ref[...], w_value_ref[:, lanes])
                for side in range(2):
                    mine = left if side == 0 else ~left
                    value_ref[2 * pair + side, rows, :128] = jnp.where(mine, values, 0.0).astype(
                        jnp.bfloat16
                    )
                    value_ref[2 * pair + side, rows, 128:] = jnp.where(mine, 1.0, 0.0).astype(
                        jnp.bfloat16
                    )
        for move in moves[2:]:
            move.wait()

    inside = None
    for pair in range(PAIRS):
        lanes = slice(128 * pair, 128 * pair + 128)
        query = query_ref[step, :, lanes]
        total = None
        for side in range(2):
            for start in range(0, ROWS, CHUNK):
                rows = slice(start, start + CHUNK)
                weights = jnp.exp2(dot(query, key_ref[2 * pair + side, :, rows]))
                part = dot(weights.astype(jnp.bfloat16), value_ref[2 * pair + side, rows])
                total = part if total is None else total + part
        sums = total[:, 128:]
        good = jnp.where((sums >= LOW) & (sums <= HIGH), 1.0, 0.0)
        inside = good if inside is None else jnp.minimum(inside, good)
        mixed_ref[:, lanes] = (total[:, :128] / sums).astype(jnp.bfloat16)

    @pl.when(jnp.min(inside) < 0.5)
    def _():
        def some_rows(strip, carry):
            rows = pl.ds(pl.multiple_of(strip * 128, 128), 128)
            for pair in range(PAIRS):
                lanes = slice(128 * pair, 128 * pair + 128)
                query = query_ref[step, rows, lanes]
                total = jnp.zeros((128, 256), jnp.float32)
                for side in range(2):
                    scores = dot(query, key_ref[2 * pair + side])
                    weights = jnp.exp2(scores - jnp.max(scores, -1, keepdims=True))
                    total += dot(weights.astype(jnp.bfloat16), value_ref[2 * pair + side])
                mixed_ref[rows, lanes] = (total[:, :128] / total[:, 128:]).astype(jnp.bfloat16)
            return carry

        lax.fori_loop(0, PIX // 128, some_rows, 0)

    projected = dot(mixed_ref[...], w_out_ref[...])
    out_ref[0] = (hidden_ref[step].astype(jnp.float32) + projected).astype(jnp.bfloat16)


def shards(
    latents,
    timestep,
    context_frame,
    gain_pre,
    w_temporal,
    w_time,
    gain_mid,
    w_query,
    w_key,
    w_value,
    w_out,
):
    up = [(i, (i + 1) % 256) for i in range(256)]
    down = [(j, i) for i, j in up]
    after = lax.ppermute(latents[:1], AXES, down)
    before = lax.ppermute(latents[1:], AXES, up)

    gain_pre = gain_pre.reshape(1, C)
    gain_mid = gain_mid.reshape(1, C)
    frame, pair, square = (PIX, C), (2, PIX, C), (C, C)
    half, single = jnp.bfloat16, jnp.float32
    mac = 2 * PIX * C * C
    here, there = pl.BlockSpec(memory_space=pltpu.VMEM), pl.BlockSpec(memory_space=pltpu.HBM)
    scalar = pl.BlockSpec(memory_space=pltpu.SMEM)
    temb = time_bias(timestep, w_time)
    part, other_part = call(
        own_taps,
        "own_taps",
        (jax.ShapeDtypeStruct(frame, single), jax.ShapeDtypeStruct(frame, single)),
        [scalar, here, here, here, there],
        (here, here),
        4 * mac,
        8 * 10**6,
        TAPS_VMEM,
        scratch_shapes=[pltpu.VMEM((2 * C, 2 * C), half), pltpu.SemaphoreType.DMA((4,))],
    )(context_frame, latents, gain_pre, temb, w_temporal)

    row = np.arange(2 * PW)
    left = np.broadcast_to((row % PW < PW // 2)[:, None], (2 * PW, C))
    sides = jnp.asarray(np.concatenate([left, ~left], axis=1), single)
    ctx = call(
        context_rows,
        "context_rows",
        jax.ShapeDtypeStruct((8, 4, C), half),
        [scalar, here, here, here, here, here, here, here],
        here,
        mac,
        8 * 10**6,
        CONTEXT_VMEM,
    )(context_frame, before, after, gain_pre, gain_mid, sides, part, w_temporal)
    hidden, query = call(
        hidden_queries,
        "hidden_queries",
        (jax.ShapeDtypeStruct(pair, half), jax.ShapeDtypeStruct(pair, half)),
        [scalar, here, here, here, here, there, there, there, there],
        (here, here),
        4 * mac,
        12 * 10**6,
        HIDDEN_VMEM,
        scratch_shapes=[
            pltpu.VMEM(pair, single),
            pltpu.VMEM(pair, half),
            pltpu.VMEM(square, half),
            pltpu.SemaphoreType.DMA((5,)),
        ],
    )(context_frame, before, after, gain_pre, gain_mid, part, other_part, w_temporal, w_query)

    line = exchange(ctx, groups_by(lambda x, y, z, core: (x, y, core))).reshape(32, C)
    plane = exchange(
        jnp.broadcast_to(line[None], (16, 32, C)), groups_by(lambda x, y, z, core: (z, core))
    ).reshape(512, C)
    plane, hidden, query = lax.optimization_barrier((plane, hidden, query))
    swapped = lax.ppermute(plane, AXES, [(i, i ^ 1) for i in range(256)])

    return call(
        attention,
        "attention",
        jax.ShapeDtypeStruct(pair, half),
        None,
        None,
        2 * 10**10,
        10 * 10**6,
        ATTENTION_VMEM,
        grid_spec=pltpu.PrefetchScalarGridSpec(
            num_scalar_prefetch=1,
            grid=(2,),
            in_specs=[whole((ROWS // 2, C))] * 2 + [there] * 5,
            out_specs=pl.BlockSpec(
                (1,) + frame, lambda i, pick: (jnp.where(pick[0] == 0, i, 1 - i), 0, 0)
            ),
            scratch_shapes=[
                pltpu.VMEM((2 * PAIRS, 128, ROWS), half),
                pltpu.VMEM((2 * PAIRS, ROWS, 256), half),
                pltpu.VMEM(frame, half),
                pltpu.VMEM(square, half),
                pltpu.VMEM(square, half),
                pltpu.VMEM(square, half),
                pltpu.VMEM(pair, half),
                pltpu.VMEM(pair, half),
                pltpu.SemaphoreType.DMA((5,)),
            ],
        ),
    )(context_frame, plane, swapped, w_key, w_value, w_out, query, hidden)


def solution(mesh):
    return jax.shard_map(
        shards,
        mesh=mesh,
        in_specs=(
            P(("clip", "group"), None, None),
            P(),
            P(("clip", "group")),
            P(),
            P(),
            P(),
            P(),
            P(),
            P(),
            P(),
            P(),
        ),
        out_specs=P(("clip", "group"), None, None),
        check_vma=False,
    )
```

```python
import functools
import math

import jax
import jax.numpy as jnp
import numpy as np
from jax import lax
from jax.experimental import pallas as pl
from jax.experimental.pallas import tpu as pltpu
from jax.sharding import PartitionSpec as P

HEAD_DIM = 64
PH = 32
PW = 20
PIX = PH * PW
C = 640
PAIRS = C // (2 * HEAD_DIM)
ROWS = 1024
ONES = 16
STRIP = 320
AXES = ("clip", "group")
MIB = 2**20
TAPS_VMEM = 24 * MIB
CONTEXT_VMEM = 24 * MIB
HIDDEN_VMEM = 56 * MIB
ATTENTION_VMEM = 52 * MIB
SCALE = math.log2(math.e) / math.sqrt(HEAD_DIM)
LOW, HIGH = 2.0**-100, 2.0**110


def place(device):
    clip, group = divmod(device, 32)
    x_low, y = divmod(clip, 4)
    x_high, rest = divmod(group, 16)
    z, core = divmod(rest, 2)
    return x_high * 2 + x_low, y, z, core


def groups_by(key):
    found = {}
    for device in range(256):
        found.setdefault(key(*place(device)), []).append(device)
    return list(found.values())


def exchange(copies, groups):
    return lax.all_to_all(copies, AXES, 0, 0, axis_index_groups=groups, tiled=False)


def dot(a, b):
    return jnp.dot(a, b, preferred_element_type=jnp.float32)


def normalize(values, gain):
    return values * lax.rsqrt(jnp.mean(values * values, -1, keepdims=True) + 1e-06) * gain


def time_bias(timestep, w_time):
    half = w_time.shape[0] // 2
    freqs = jnp.exp(-math.log(10000.0) * jnp.arange(half, dtype=jnp.float32) / half)
    angle = timestep.astype(jnp.float32)[0] * freqs
    embed = jnp.concatenate([jnp.cos(angle), jnp.sin(angle)])
    return jnp.dot(
        jax.nn.silu(embed)[None, :],
        w_time,
        precision=lax.Precision.HIGHEST,
        preferred_element_type=jnp.float32,
    )


def call(kernel, name, out_shape, in_specs, out_specs, flops, moved, vmem, **kwargs):
    return pl.pallas_call(
        kernel,
        out_shape=out_shape,
        in_specs=in_specs,
        out_specs=out_specs,
        name=name,
        compiler_params=pltpu.CompilerParams(vmem_limit_bytes=vmem),
        cost_estimate=pl.CostEstimate(flops=flops, bytes_accessed=moved, transcendentals=0),
        **kwargs,
    )


def copy_all(pairs, sems):
    copies = [pltpu.make_async_copy(a, b, sems.at[i]) for i, (a, b) in enumerate(pairs)]
    for copy in copies:
        copy.start()
    return copies


def strips():
    return [slice(start, start + STRIP) for start in range(0, PIX, STRIP)]


def own_taps(
    pick_ref, latents_ref, gain_ref, temb_ref, taps_ref, soon_ref, chosen_ref, other_ref, big_ref, sems
):
    first = pick_ref[0] == 0
    order = ((1, 0), (2, 1))
    copies = copy_all(
        [
            (taps_ref.at[order[i][j]], big_ref.at[pl.ds(C * i, C), pl.ds(C * j, C)])
            for i in range(2)
            for j in range(2)
        ],
        sems,
    )
    gain, temb = gain_ref[...], temb_ref[...]
    for copy in copies:
        copy.wait()
    for rows in strips():
        source = [latents_ref[f, rows].astype(jnp.float32) for f in range(2)]
        norm = jnp.concatenate([normalize(s, gain).astype(jnp.bfloat16) for s in source], axis=1)
        both = dot(norm, big_ref[...])
        parts = [source[f] + temb + both[:, C * f : C * f + C] for f in range(2)]
        chosen = jnp.where(first, parts[0], parts[1])
        soon_ref[rows] = chosen
        chosen_ref[rows] = chosen
        other_ref[rows] = jnp.where(first, parts[1], parts[0])


def context_rows(
    pick_ref, before_ref, after_ref, gain_pre_ref, gain_mid_ref, side_ref, part_ref, taps_ref, ctx_ref
):
    first = pick_ref[0] == 0
    tap = jnp.where(first, 0, 2)
    gain_pre, gain_mid = gain_pre_ref[...], gain_mid_ref[...]
    tile = side_ref.shape[0]
    sums = []
    for half in range(2):
        rows = slice(half * PIX // 2, (half + 1) * PIX // 2)
        halo = jnp.where(first, before_ref[0, rows], after_ref[0, rows]).astype(jnp.float32)
        norm = normalize(halo, gain_pre).astype(jnp.bfloat16)
        hidden = (part_ref[rows] + dot(norm, taps_ref[tap])).astype(jnp.bfloat16)
        norm = normalize(hidden.astype(jnp.float32), gain_mid).astype(jnp.bfloat16)
        norm = norm.astype(jnp.float32).reshape(PIX // 2 // tile, tile, C)
        for side in range(2):
            here = jnp.sum(norm * side_ref[:, C * side : C * side + C], axis=0)
            sums.append(jnp.sum(here, axis=0, keepdims=True))
    pooled = jnp.concatenate(sums, axis=0) * (4.0 / PIX)
    rows = normalize(pooled, 1.0).astype(jnp.bfloat16)
    for copy in range(ctx_ref.shape[0]):
        ctx_ref[copy] = rows


def hidden_queries(
    slot, pick_ref, before_ref, after_ref, gain_pre_ref, gain_mid_ref, part_hbm, taps_hbm, w_query_hbm,
    hidden_ref, query_ref, part_ref, tap_ref, w_query_ref, sems,
):
    first = (pick_ref[0] == 0) == (slot == 0)
    copies = copy_all(
        [
            (taps_hbm.at[jnp.where(first, 0, 2)], tap_ref),
            (part_hbm, part_ref),
            (w_query_hbm, w_query_ref),
        ],
        sems,
    )
    gain_pre, gain_mid = gain_pre_ref[...], gain_mid_ref[...]
    for copy in copies:
        copy.wait()
    halo = jnp.where(first, before_ref[0], after_ref[0]).astype(jnp.float32)
    norm = normalize(halo, gain_pre).astype(jnp.bfloat16)
    hidden = (part_ref[...] + dot(norm, tap_ref[...])).astype(jnp.bfloat16)
    hidden_ref[...] = hidden
    norm = normalize(hidden.astype(jnp.float32), gain_mid).astype(jnp.bfloat16)
    query_ref[...] = (dot(norm, w_query_ref[...]) * SCALE).T.astype(jnp.bfloat16)


def pair_rows(pair):
    return pl.ds(pl.multiple_of(128 * pair, 128), 128)


def attention(
    pick_ref, near_ref, far_ref, w_key_hbm, w_value_hbm, w_out_hbm, query_0, query_1, hidden_0,
    hidden_1, out_hbm, key_ref, value_ref, mixed_ref, w_both_ref, w_out_ref, query_ref, hidden_ref,
    out_ref, sems, out_sems,
):
    half = ROWS // 2
    moves = copy_all(
        [
            (source.at[:, pl.ds(128 * pair, 128)], w_both_ref.at[:, pl.ds(256 * pair + place, 128)])
            for pair in range(PAIRS)
            for source, place in ((w_key_hbm, 0), (w_value_hbm, 128))
        ]
        + [
            (query_0, query_ref.at[0]),
            (query_1, query_ref.at[1]),
            (w_out_hbm, w_out_ref),
            (hidden_0, hidden_ref.at[0]),
            (hidden_1, hidden_ref.at[1]),
        ],
        sems,
    )

    def context(pair, slot):
        lanes = pl.ds(pl.multiple_of(256 * pair, 256), 256)
        left = lax.broadcasted_iota(jnp.int32, (half, 128), 1) < HEAD_DIM
        for number, ctx_ref in enumerate((near_ref, far_ref)):
            rows = slice(half * number, half * number + half)
            both = dot(ctx_ref[...], w_both_ref[:, lanes])
            keys, values = both[:, :128], both[:, 128:].T.astype(jnp.bfloat16)
            for side in range(2):
                mine = left if side == 0 else ~left
                key_ref[slot, side, rows] = jnp.where(mine, keys, 0.0).astype(jnp.bfloat16)
                value_ref[slot, side, :HEAD_DIM, rows] = values[HEAD_DIM * side :][:HEAD_DIM]

    def project(frame):
        projected = dot(mixed_ref[frame].T, w_out_ref[...])
        out = (hidden_ref[frame].astype(jnp.float32) + projected).astype(jnp.bfloat16)
        out_ref[frame] = out
        place = jnp.where(pick_ref[0] == 0, frame, 1 - frame)
        return copy_all([(out_ref.at[frame], out_hbm.at[place])], out_sems.at[pl.ds(frame, 1)])

    moves, late = moves[: 2 * PAIRS], moves[2 * PAIRS :]
    value_ref[:, :, HEAD_DIM:] = jnp.ones((2, 2, ONES, ROWS), jnp.bfloat16)
    for move in moves + late[:2]:
        move.wait()
    inside = None
    context(0, 0)
    for pair in range(PAIRS):
        if pair + 1 < PAIRS:
            context(pair + 1, (pair + 1) % 2)
        for frame in range(2):
            for side in range(2):
                scores = dot(key_ref[pair % 2, side], query_ref[frame, 128 * pair : 128 * pair + 128])
                weights = jnp.exp2(scores).astype(jnp.bfloat16)
                total = dot(value_ref[pair % 2, side], weights)
                sums = total[HEAD_DIM : HEAD_DIM + 1]
                good = jnp.where((sums >= LOW) & (sums <= HIGH), 1.0, 0.0)
                inside = good if inside is None else jnp.minimum(inside, good)
                head = HEAD_DIM * (2 * pair + side)
                mixed = total[:HEAD_DIM] * (1.0 / sums)
                mixed_ref[frame, head : head + HEAD_DIM] = mixed.astype(jnp.bfloat16)
    for move in late[2:]:
        move.wait()
    writes = project(0) + project(1)
    worst = jnp.min(inside)
    for write in writes:
        write.wait()

    @pl.when(worst < 0.5)
    def _():
        def some_pixels(strip, pair):
            pixels = pl.ds(pl.multiple_of(strip * 128, 128), 128)
            for frame in range(2):
                query = query_ref[frame, pair_rows(pair), pixels]
                for side in range(2):
                    scores = dot(key_ref[0, side], query)
                    weights = jnp.exp2(scores - jnp.max(scores, 0, keepdims=True))
                    total = dot(value_ref[0, side], weights.astype(jnp.bfloat16))
                    mixed = total[:HEAD_DIM] * (1.0 / total[HEAD_DIM : HEAD_DIM + 1])
                    rows = pl.ds(pl.multiple_of(128 * pair + HEAD_DIM * side, HEAD_DIM), HEAD_DIM)
                    mixed_ref[frame, rows, pixels] = mixed.astype(jnp.bfloat16)
            return pair

        def one_pair(pair, carry):
            context(pair, 0)
            lax.fori_loop(0, PIX // 128, some_pixels, pair)
            return carry

        lax.fori_loop(0, PAIRS, one_pair, 0)
        for write in project(0) + project(1):
            write.wait()


def attend(*operands):
    frame, pair, square, half = (PIX, C), (2, PIX, C), (C, C), jnp.bfloat16
    here, there = pl.BlockSpec(memory_space=pltpu.VMEM), pl.BlockSpec(memory_space=pltpu.HBM)
    return call(
        attention,
        "attention",
        jax.ShapeDtypeStruct(pair, half),
        [pl.BlockSpec(memory_space=pltpu.SMEM), here, here] + [there] * 7,
        there,
        2 * 10**10,
        10 * 10**6,
        ATTENTION_VMEM,
        scratch_shapes=[
            pltpu.VMEM((2, 2, ROWS, 128), half),
            pltpu.VMEM((2, 2, HEAD_DIM + ONES, ROWS), half),
            pltpu.VMEM(pair, half),
            pltpu.VMEM((C, 2 * C), half),
            pltpu.VMEM(square, half),
            pltpu.VMEM(pair, half),
            pltpu.VMEM(pair, half),
            pltpu.VMEM(pair, half),
            pltpu.SemaphoreType.DMA((2 * PAIRS + 5,)),
            pltpu.SemaphoreType.DMA((2,)),
        ],
    )(*operands)


def shards(
    latents,
    timestep,
    context_frame,
    gain_pre,
    w_temporal,
    w_time,
    gain_mid,
    w_query,
    w_key,
    w_value,
    w_out,
):
    up = [(i, (i + 1) % 256) for i in range(256)]
    down = [(j, i) for i, j in up]
    after = lax.ppermute(latents[:1], AXES, down)
    before = lax.ppermute(latents[1:], AXES, up)

    gain_pre = gain_pre.reshape(1, C)
    gain_mid = gain_mid.reshape(1, C)
    frame, pair, square = (PIX, C), (2, PIX, C), (C, C)
    half, single = jnp.bfloat16, jnp.float32
    mac = 2 * PIX * C * C
    here, there = pl.BlockSpec(memory_space=pltpu.VMEM), pl.BlockSpec(memory_space=pltpu.HBM)
    scalar = pl.BlockSpec(memory_space=pltpu.SMEM)
    temb = time_bias(timestep, w_time)
    soon_part, part, other_part = call(
        own_taps,
        "own_taps",
        (jax.ShapeDtypeStruct(frame, single),) * 3,
        [scalar, here, here, here, there],
        (here, here, here),
        4 * mac,
        8 * 10**6,
        TAPS_VMEM,
        scratch_shapes=[pltpu.VMEM((2 * C, 2 * C), half), pltpu.SemaphoreType.DMA((4,))],
    )(context_frame, latents, gain_pre, temb, w_temporal)

    row = np.arange(2 * PW)
    left = np.broadcast_to((row % PW < PW // 2)[:, None], (2 * PW, C))
    sides = jnp.asarray(np.concatenate([left, ~left], axis=1), single)
    ctx = call(
        context_rows,
        "context_rows",
        jax.ShapeDtypeStruct((8, 4, C), half),
        [scalar, here, here, here, here, here, here, here],
        here,
        mac,
        8 * 10**6,
        CONTEXT_VMEM,
    )(context_frame, before, after, gain_pre, gain_mid, sides, soon_part, w_temporal)
    def frame_call(slot, frame_part):
        return call(
            functools.partial(hidden_queries, slot),
            "hidden_queries",
            (jax.ShapeDtypeStruct(frame, half), jax.ShapeDtypeStruct(frame, half)),
            [scalar, here, here, here, here, there, there, there],
            (here, here),
            2 * mac,
            6 * 10**6,
            HIDDEN_VMEM,
            scratch_shapes=[
                pltpu.VMEM(frame, single),
                pltpu.VMEM(square, half),
                pltpu.VMEM(square, half),
                pltpu.SemaphoreType.DMA((3,)),
            ],
        )(context_frame, before, after, gain_pre, gain_mid, frame_part, w_temporal, w_query)

    line = exchange(ctx, groups_by(lambda x, y, z, core: (x, y, core))).reshape(32, C)
    hidden_0, query_0 = frame_call(0, part)
    line, hidden_0, query_0 = lax.optimization_barrier((line, hidden_0, query_0))
    plane = exchange(
        jnp.broadcast_to(line[None], (16, 32, C)), groups_by(lambda x, y, z, core: (z, core))
    ).reshape(512, C)
    hidden_1, query_1 = frame_call(1, other_part)
    plane, hidden_1, query_1 = lax.optimization_barrier((plane, hidden_1, query_1))
    swapped = lax.ppermute(plane, AXES, [(i, i ^ 1) for i in range(256)])

    return attend(
        context_frame, plane, swapped, w_key, w_value, w_out, query_0, query_1, hidden_0, hidden_1
    )


def solution(mesh):
    return jax.shard_map(
        shards,
        mesh=mesh,
        in_specs=(
            P(("clip", "group"), None, None),
            P(),
            P(("clip", "group")),
            P(),
            P(),
            P(),
            P(),
            P(),
            P(),
            P(),
            P(),
        ),
        out_specs=P(("clip", "group"), None, None),
        check_vma=False,
    )
```

```python
import functools
import math

import jax
import jax.numpy as jnp
import numpy as np
from jax import lax
from jax.experimental import pallas as pl
from jax.experimental.pallas import tpu as pltpu
from jax.sharding import PartitionSpec as P

HEAD_DIM = 64
PH = 32
PW = 20
PIX = PH * PW
C = 640
PAIRS = C // (2 * HEAD_DIM)
ROWS = 1024
ONES = 16
PARTS = (slice(0, 384), slice(384, PIX))
STRIP = 320
AXES = ("clip", "group")
MIB = 2**20
TAPS_VMEM = 24 * MIB
CONTEXT_VMEM = 24 * MIB
HIDDEN_VMEM = 56 * MIB
ATTENTION_VMEM = 52 * MIB
SCALE = math.log2(math.e) / math.sqrt(HEAD_DIM)
LOW, HIGH = 2.0**-100, 2.0**110


def place(device):
    clip, group = divmod(device, 32)
    x_low, y = divmod(clip, 4)
    x_high, rest = divmod(group, 16)
    z, core = divmod(rest, 2)
    return x_high * 2 + x_low, y, z, core


def groups_by(key):
    found = {}
    for device in range(256):
        found.setdefault(key(*place(device)), []).append(device)
    return list(found.values())


def exchange(copies, groups):
    return lax.all_to_all(copies, AXES, 0, 0, axis_index_groups=groups, tiled=False)


def dot(a, b):
    return jnp.dot(a, b, preferred_element_type=jnp.float32)


def normalize(values, gain):
    return values * lax.rsqrt(jnp.mean(values * values, -1, keepdims=True) + 1e-06) * gain


def time_bias(timestep, w_time):
    half = w_time.shape[0] // 2
    freqs = jnp.exp(-math.log(10000.0) * jnp.arange(half, dtype=jnp.float32) / half)
    angle = timestep.astype(jnp.float32)[0] * freqs
    embed = jnp.concatenate([jnp.cos(angle), jnp.sin(angle)])
    return jnp.dot(
        jax.nn.silu(embed)[None, :],
        w_time,
        precision=lax.Precision.HIGHEST,
        preferred_element_type=jnp.float32,
    )


def call(kernel, name, out_shape, in_specs, out_specs, flops, moved, vmem, **kwargs):
    return pl.pallas_call(
        kernel,
        out_shape=out_shape,
        in_specs=in_specs,
        out_specs=out_specs,
        name=name,
        compiler_params=pltpu.CompilerParams(vmem_limit_bytes=vmem),
        cost_estimate=pl.CostEstimate(flops=flops, bytes_accessed=moved, transcendentals=0),
        **kwargs,
    )


def copy_all(pairs, sems):
    copies = [pltpu.make_async_copy(a, b, sems.at[i]) for i, (a, b) in enumerate(pairs)]
    for copy in copies:
        copy.start()
    return copies


def strips():
    return [slice(start, start + STRIP) for start in range(0, PIX, STRIP)]


def own_taps(
    pick_ref, latents_ref, gain_ref, temb_ref, taps_ref, soon_ref, chosen_ref, other_ref, big_ref, sems
):
    first = pick_ref[0] == 0
    order = ((1, 0), (2, 1))
    copies = copy_all(
        [
            (taps_ref.at[order[i][j]], big_ref.at[pl.ds(C * i, C), pl.ds(C * j, C)])
            for i in range(2)
            for j in range(2)
        ],
        sems,
    )
    gain, temb = gain_ref[...], temb_ref[...]
    for copy in copies:
        copy.wait()
    for rows in strips():
        source = [latents_ref[f, rows].astype(jnp.float32) for f in range(2)]
        norm = jnp.concatenate([normalize(s, gain).astype(jnp.bfloat16) for s in source], axis=1)
        both = dot(norm, big_ref[...])
        parts = [source[f] + temb + both[:, C * f : C * f + C] for f in range(2)]
        chosen = jnp.where(first, parts[0], parts[1])
        soon_ref[rows] = chosen
        chosen_ref[rows] = chosen
        other_ref[rows] = jnp.where(first, parts[1], parts[0])


def context_rows(
    pick_ref, apart_ref, beside_ref, beyond_ref, gain_pre_ref, gain_mid_ref, side_ref, part_ref,
    taps_ref, ctx_ref,
):
    tap = jnp.where(pick_ref[0] == 0, 0, 2)
    far = apart_ref[0] == 1
    gain_pre, gain_mid = gain_pre_ref[...], gain_mid_ref[...]
    tile = side_ref.shape[0]
    sums = []
    for half in range(2):
        rows = slice(half * PIX // 2, (half + 1) * PIX // 2)
        halo = jnp.where(far, beyond_ref[0, rows], beside_ref[0, rows]).astype(jnp.float32)
        norm = normalize(halo, gain_pre).astype(jnp.bfloat16)
        hidden = (part_ref[rows] + dot(norm, taps_ref[tap])).astype(jnp.bfloat16)
        norm = normalize(hidden.astype(jnp.float32), gain_mid).astype(jnp.bfloat16)
        norm = norm.astype(jnp.float32).reshape(PIX // 2 // tile, tile, C)
        for side in range(2):
            here = jnp.sum(norm * side_ref[:, C * side : C * side + C], axis=0)
            sums.append(jnp.sum(here, axis=0, keepdims=True))
    pooled = jnp.concatenate(sums, axis=0) * (4.0 / PIX)
    rows = normalize(pooled, 1.0).astype(jnp.bfloat16)
    for copy in range(ctx_ref.shape[0]):
        ctx_ref[copy] = rows


def hidden_queries(
    slot, pick_ref, apart_ref, gain_pre_ref, gain_mid_ref, beside_hbm, beyond_hbm, part_hbm, taps_hbm,
    w_query_hbm, hidden_hbm, query_hbm, halo_ref, part_ref, tap_ref, w_query_ref, hidden_ref, query_ref, sems,
    out_sems,
):
    tap = jnp.where((pick_ref[0] == 0) == (slot == 0), 0, 2)
    far = (apart_ref[0] == 1) == (slot == 0)
    halo_copy = pltpu.make_async_copy(beyond_hbm.at[0], halo_ref, sems.at[3])
    pl.when(far)(halo_copy.start)
    pl.when(~far)(pltpu.make_async_copy(beside_hbm.at[0], halo_ref, sems.at[3]).start)
    tap_copy, part_copy, query_copy = copy_all(
        [
            (taps_hbm.at[tap], tap_ref),
            (part_hbm, part_ref),
            (w_query_hbm, w_query_ref),
        ],
        sems,
    )
    gain_pre, gain_mid = gain_pre_ref[...], gain_mid_ref[...]
    halo_copy.wait()
    norm = normalize(halo_ref[...].astype(jnp.float32), gain_pre).astype(jnp.bfloat16)
    tap_copy.wait()
    part_copy.wait()
    query_copy.wait()
    for rows in PARTS:
        hidden = (part_ref[rows] + dot(norm[rows], tap_ref[...])).astype(jnp.bfloat16)
        hidden_ref[rows] = hidden
        later = normalize(hidden.astype(jnp.float32), gain_mid).astype(jnp.bfloat16)
        query_ref[:, rows] = (dot(later, w_query_ref[...]) * SCALE).T.astype(jnp.bfloat16)
    for copy in copy_all([(hidden_ref, hidden_hbm), (query_ref, query_hbm)], out_sems):
        copy.wait()


def pair_rows(pair):
    return pl.ds(pl.multiple_of(128 * pair, 128), 128)


def attention(
    pick_ref, near_ref, far_ref, w_key_hbm, w_value_hbm, w_out_hbm, query_0, query_1, hidden_0,
    hidden_1, out_hbm, key_ref, value_ref, mixed_ref, w_both_ref, w_out_ref, query_ref, hidden_ref,
    out_ref, sems, out_sems,
):
    half = ROWS // 2
    moves = copy_all(
        [
            (source.at[:, pl.ds(128 * pair, 128)], w_both_ref.at[:, pl.ds(256 * pair + place, 128)])
            for pair in range(PAIRS)
            for source, place in ((w_key_hbm, 0), (w_value_hbm, 128))
        ]
        + [
            (query_0, query_ref.at[0]),
            (query_1, query_ref.at[1]),
            (w_out_hbm, w_out_ref),
            (hidden_0, hidden_ref.at[0]),
            (hidden_1, hidden_ref.at[1]),
        ],
        sems,
    )

    def context(pair, slot):
        lanes = pl.ds(pl.multiple_of(256 * pair, 256), 256)
        left = lax.broadcasted_iota(jnp.int32, (half, 128), 1) < HEAD_DIM
        for number, ctx_ref in enumerate((near_ref, far_ref)):
            rows = slice(half * number, half * number + half)
            both = dot(ctx_ref[...], w_both_ref[:, lanes])
            keys, values = both[:, :128], both[:, 128:].T.astype(jnp.bfloat16)
            for side in range(2):
                mine = left if side == 0 else ~left
                key_ref[slot, side, rows] = jnp.where(mine, keys, 0.0).astype(jnp.bfloat16)
                value_ref[slot, side, :HEAD_DIM, rows] = values[HEAD_DIM * side :][:HEAD_DIM]

    def project(frame):
        projected = dot(mixed_ref[frame].T, w_out_ref[...])
        out = (hidden_ref[frame].astype(jnp.float32) + projected).astype(jnp.bfloat16)
        out_ref[frame] = out
        place = jnp.where(pick_ref[0] == 0, frame, 1 - frame)
        return copy_all([(out_ref.at[frame], out_hbm.at[place])], out_sems.at[pl.ds(frame, 1)])

    moves, late = moves[: 2 * PAIRS], moves[2 * PAIRS :]
    value_ref[:, :, HEAD_DIM:] = jnp.ones((2, 2, ONES, ROWS), jnp.bfloat16)
    for move in moves + late[:2]:
        move.wait()
    inside = None
    context(0, 0)
    for pair in range(PAIRS):
        if pair + 1 < PAIRS:
            context(pair + 1, (pair + 1) % 2)
        for frame in range(2):
            for side in range(2):
                scores = dot(key_ref[pair % 2, side], query_ref[frame, 128 * pair : 128 * pair + 128])
                weights = jnp.exp2(scores).astype(jnp.bfloat16)
                total = dot(value_ref[pair % 2, side], weights)
                sums = total[HEAD_DIM : HEAD_DIM + 1]
                good = jnp.where((sums >= LOW) & (sums <= HIGH), 1.0, 0.0)
                inside = good if inside is None else jnp.minimum(inside, good)
                head = HEAD_DIM * (2 * pair + side)
                mixed = total[:HEAD_DIM] * (1.0 / sums)
                mixed_ref[frame, head : head + HEAD_DIM] = mixed.astype(jnp.bfloat16)
    for move in late[2:]:
        move.wait()
    writes = project(0) + project(1)
    worst = jnp.min(inside)
    for write in writes:
        write.wait()

    @pl.when(worst < 0.5)
    def _():
        def some_pixels(strip, pair):
            pixels = pl.ds(pl.multiple_of(strip * 128, 128), 128)
            for frame in range(2):
                query = query_ref[frame, pair_rows(pair), pixels]
                for side in range(2):
                    scores = dot(key_ref[0, side], query)
                    weights = jnp.exp2(scores - jnp.max(scores, 0, keepdims=True))
                    total = dot(value_ref[0, side], weights.astype(jnp.bfloat16))
                    mixed = total[:HEAD_DIM] * (1.0 / total[HEAD_DIM : HEAD_DIM + 1])
                    rows = pl.ds(pl.multiple_of(128 * pair + HEAD_DIM * side, HEAD_DIM), HEAD_DIM)
                    mixed_ref[frame, rows, pixels] = mixed.astype(jnp.bfloat16)
            return pair

        def one_pair(pair, carry):
            context(pair, 0)
            lax.fori_loop(0, PIX // 128, some_pixels, pair)
            return carry

        lax.fori_loop(0, PAIRS, one_pair, 0)
        for write in project(0) + project(1):
            write.wait()


def attend(*operands):
    frame, pair, square, half = (PIX, C), (2, PIX, C), (C, C), jnp.bfloat16
    here, there = pl.BlockSpec(memory_space=pltpu.VMEM), pl.BlockSpec(memory_space=pltpu.HBM)
    return call(
        attention,
        "attention",
        jax.ShapeDtypeStruct(pair, half),
        [pl.BlockSpec(memory_space=pltpu.SMEM), here, here] + [there] * 7,
        there,
        2 * 10**10,
        10 * 10**6,
        ATTENTION_VMEM,
        scratch_shapes=[
            pltpu.VMEM((2, 2, ROWS, 128), half),
            pltpu.VMEM((2, 2, HEAD_DIM + ONES, ROWS), half),
            pltpu.VMEM(pair, half),
            pltpu.VMEM((C, 2 * C), half),
            pltpu.VMEM(square, half),
            pltpu.VMEM(pair, half),
            pltpu.VMEM(pair, half),
            pltpu.VMEM(pair, half),
            pltpu.SemaphoreType.DMA((2 * PAIRS + 5,)),
            pltpu.SemaphoreType.DMA((2,)),
        ],
    )(*operands)


def shards(
    latents,
    timestep,
    context_frame,
    gain_pre,
    w_temporal,
    w_time,
    gain_mid,
    w_query,
    w_key,
    w_value,
    w_out,
):
    core = lax.axis_index("group") % 2
    pick = jnp.where(context_frame == 0, 0, 1)
    apart = jnp.where(pick == core, 1, 0)
    abroad = [(i, (i + 1) % 256 if i % 2 else (i - 1) % 256) for i in range(256)]
    beyond = lax.ppermute(lax.dynamic_slice_in_dim(latents, core, 1, 0), AXES, abroad)
    beside = lax.ppermute(
        lax.dynamic_slice_in_dim(latents, 1 - core, 1, 0), AXES, [(i, i ^ 1) for i in range(256)]
    )

    gain_pre = gain_pre.reshape(1, C)
    gain_mid = gain_mid.reshape(1, C)
    frame, pair, square = (PIX, C), (2, PIX, C), (C, C)
    half, single = jnp.bfloat16, jnp.float32
    mac = 2 * PIX * C * C
    here, there = pl.BlockSpec(memory_space=pltpu.VMEM), pl.BlockSpec(memory_space=pltpu.HBM)
    scalar = pl.BlockSpec(memory_space=pltpu.SMEM)
    temb = time_bias(timestep, w_time)
    soon_part, part, other_part = call(
        own_taps,
        "own_taps",
        (jax.ShapeDtypeStruct(frame, single),) * 3,
        [scalar, here, here, here, there],
        (here, here, here),
        4 * mac,
        8 * 10**6,
        TAPS_VMEM,
        scratch_shapes=[pltpu.VMEM((2 * C, 2 * C), half), pltpu.SemaphoreType.DMA((4,))],
    )(pick, latents, gain_pre, temb, w_temporal)

    row = np.arange(2 * PW)
    left = np.broadcast_to((row % PW < PW // 2)[:, None], (2 * PW, C))
    sides = jnp.asarray(np.concatenate([left, ~left], axis=1), single)
    ctx = call(
        context_rows,
        "context_rows",
        jax.ShapeDtypeStruct((8, 4, C), half),
        [scalar, scalar, here, here, here, here, here, here, here],
        here,
        mac,
        8 * 10**6,
        CONTEXT_VMEM,
    )(pick, apart, beside, beyond, gain_pre, gain_mid, sides, soon_part, w_temporal)
    def frame_call(slot, frame_part):
        return call(
            functools.partial(hidden_queries, slot),
            "hidden_queries",
            (jax.ShapeDtypeStruct(frame, half), jax.ShapeDtypeStruct(frame, half)),
            [scalar, scalar, here, here, there, there, there, there, there],
            (there, there),
            2 * mac,
            6 * 10**6,
            HIDDEN_VMEM,
            scratch_shapes=[
                pltpu.VMEM(frame, half),
                pltpu.VMEM(frame, single),
                pltpu.VMEM(square, half),
                pltpu.VMEM(square, half),
                pltpu.VMEM(frame, half),
                pltpu.VMEM(frame, half),
                pltpu.SemaphoreType.DMA((4,)),
                pltpu.SemaphoreType.DMA((2,)),
            ],
        )(pick, apart, gain_pre, gain_mid, beside, beyond, frame_part, w_temporal, w_query)

    line = exchange(ctx, groups_by(lambda x, y, z, core: (x, y, core))).reshape(32, C)
    hidden_0, query_0 = frame_call(0, part)
    line, hidden_0, query_0 = lax.optimization_barrier((line, hidden_0, query_0))
    plane = exchange(
        jnp.broadcast_to(line[None], (16, 32, C)), groups_by(lambda x, y, z, core: (z, core))
    ).reshape(512, C)
    hidden_1, query_1 = frame_call(1, other_part)
    plane, hidden_1, query_1 = lax.optimization_barrier((plane, hidden_1, query_1))
    swapped = lax.ppermute(plane, AXES, [(i, i ^ 1) for i in range(256)])

    return attend(
        pick, plane, swapped, w_key, w_value, w_out, query_0, query_1, hidden_0, hidden_1
    )


def solution(mesh):
    return jax.shard_map(
        shards,
        mesh=mesh,
        in_specs=(
            P(("clip", "group"), None, None),
            P(),
            P(("clip", "group")),
            P(),
            P(),
            P(),
            P(),
            P(),
            P(),
            P(),
            P(),
        ),
        out_specs=P(("clip", "group"), None, None),
        check_vma=False,
    )
```

```python
import functools
import math

import jax
import jax.numpy as jnp
import numpy as np
from jax import lax
from jax.experimental import pallas as pl
from jax.experimental.pallas import tpu as pltpu
from jax.sharding import PartitionSpec as P

HEAD_DIM = 64
PH = 32
PW = 20
PIX = PH * PW
C = 640
PAIRS = C // (2 * HEAD_DIM)
ROWS = 1024
ONES = 16
PARTS = (slice(0, 384), slice(384, PIX))
STRIP = 320
AXES = ("clip", "group")
MIB = 2**20
TAPS_VMEM = 24 * MIB
CONTEXT_VMEM = 24 * MIB
HIDDEN_VMEM = 56 * MIB
ATTENTION_VMEM = 52 * MIB
SCALE = math.log2(math.e) / math.sqrt(HEAD_DIM)
LOW, HIGH = 2.0**-100, 2.0**110


def place(device):
    clip, group = divmod(device, 32)
    x_low, y = divmod(clip, 4)
    x_high, rest = divmod(group, 16)
    z, core = divmod(rest, 2)
    return x_high * 2 + x_low, y, z, core


def groups_by(key):
    found = {}
    for device in range(256):
        found.setdefault(key(*place(device)), []).append(device)
    return list(found.values())


def exchange(copies, groups):
    return lax.all_to_all(copies, AXES, 0, 0, axis_index_groups=groups, tiled=False)


def dot(a, b):
    return jnp.dot(a, b, preferred_element_type=jnp.float32)


def normalize(values, gain):
    return values * lax.rsqrt(jnp.mean(values * values, -1, keepdims=True) + 1e-06) * gain


def time_bias(timestep, w_time):
    half = w_time.shape[0] // 2
    freqs = jnp.exp(-math.log(10000.0) * jnp.arange(half, dtype=jnp.float32) / half)
    angle = timestep.astype(jnp.float32)[0] * freqs
    embed = jnp.concatenate([jnp.cos(angle), jnp.sin(angle)])
    return jnp.dot(
        jax.nn.silu(embed)[None, :],
        w_time,
        precision=lax.Precision.HIGHEST,
        preferred_element_type=jnp.float32,
    )


def call(kernel, name, out_shape, in_specs, out_specs, flops, moved, vmem, **kwargs):
    return pl.pallas_call(
        kernel,
        out_shape=out_shape,
        in_specs=in_specs,
        out_specs=out_specs,
        name=name,
        compiler_params=pltpu.CompilerParams(vmem_limit_bytes=vmem),
        cost_estimate=pl.CostEstimate(flops=flops, bytes_accessed=moved, transcendentals=0),
        **kwargs,
    )


def copy_all(pairs, sems):
    copies = [pltpu.make_async_copy(a, b, sems.at[i]) for i, (a, b) in enumerate(pairs)]
    for copy in copies:
        copy.start()
    return copies


def strips():
    return [slice(start, start + STRIP) for start in range(0, PIX, STRIP)]


def own_taps(
    pick_ref, latents_ref, gain_ref, temb_ref, taps_ref, soon_ref, chosen_ref, other_ref, big_ref, sems
):
    first = pick_ref[0] == 0
    order = ((1, 0), (2, 1))
    copies = copy_all(
        [
            (taps_ref.at[order[i][j]], big_ref.at[pl.ds(C * i, C), pl.ds(C * j, C)])
            for i in range(2)
            for j in range(2)
        ],
        sems,
    )
    gain, temb = gain_ref[...], temb_ref[...]
    for copy in copies:
        copy.wait()
    for rows in strips():
        source = [latents_ref[f, rows].astype(jnp.float32) for f in range(2)]
        norm = jnp.concatenate([normalize(s, gain).astype(jnp.bfloat16) for s in source], axis=1)
        both = dot(norm, big_ref[...])
        parts = [source[f] + temb + both[:, C * f : C * f + C] for f in range(2)]
        chosen = jnp.where(first, parts[0], parts[1])
        soon_ref[rows] = chosen
        chosen_ref[rows] = chosen
        other_ref[rows] = jnp.where(first, parts[1], parts[0])


def context_rows(
    pick_ref, apart_ref, beside_ref, beyond_ref, gain_pre_ref, gain_mid_ref, side_ref, part_ref,
    taps_ref, ctx_ref,
):
    tap = jnp.where(pick_ref[0] == 0, 0, 2)
    far = apart_ref[0] == 1
    gain_pre, gain_mid = gain_pre_ref[...], gain_mid_ref[...]
    tile = side_ref.shape[0]
    sums = []
    for half in range(2):
        rows = slice(half * PIX // 2, (half + 1) * PIX // 2)
        halo = jnp.where(far, beyond_ref[0, rows], beside_ref[0, rows]).astype(jnp.float32)
        norm = normalize(halo, gain_pre).astype(jnp.bfloat16)
        hidden = (part_ref[rows] + dot(norm, taps_ref[tap])).astype(jnp.bfloat16)
        norm = normalize(hidden.astype(jnp.float32), gain_mid).astype(jnp.bfloat16)
        norm = norm.astype(jnp.float32).reshape(PIX // 2 // tile, tile, C)
        for side in range(2):
            here = jnp.sum(norm * side_ref[:, C * side : C * side + C], axis=0)
            sums.append(jnp.sum(here, axis=0, keepdims=True))
    pooled = jnp.concatenate(sums, axis=0) * (4.0 / PIX)
    rows = normalize(pooled, 1.0).astype(jnp.bfloat16)
    for copy in range(ctx_ref.shape[0]):
        ctx_ref[copy] = rows


def hidden_queries(
    slot, pick_ref, apart_ref, gain_pre_ref, gain_mid_ref, beside_hbm, beyond_hbm, part_hbm, taps_hbm,
    w_query_hbm, hidden_hbm, query_hbm, halo_ref, part_ref, tap_ref, w_query_ref, hidden_ref, query_ref, sems,
    out_sems,
):
    tap = jnp.where((pick_ref[0] == 0) == (slot == 0), 0, 2)
    far = (apart_ref[0] == 1) == (slot == 0)
    halo_copy = pltpu.make_async_copy(beyond_hbm.at[0], halo_ref, sems.at[3])
    pl.when(far)(halo_copy.start)
    pl.when(~far)(pltpu.make_async_copy(beside_hbm.at[0], halo_ref, sems.at[3]).start)
    tap_copy, part_copy, query_copy = copy_all(
        [
            (taps_hbm.at[tap], tap_ref),
            (part_hbm, part_ref),
            (w_query_hbm, w_query_ref),
        ],
        sems,
    )
    gain_pre, gain_mid = gain_pre_ref[...], gain_mid_ref[...]
    halo_copy.wait()
    norm = normalize(halo_ref[...].astype(jnp.float32), gain_pre).astype(jnp.bfloat16)
    tap_copy.wait()
    part_copy.wait()
    query_copy.wait()
    for rows in PARTS:
        hidden = (part_ref[rows] + dot(norm[rows], tap_ref[...])).astype(jnp.bfloat16)
        hidden_ref[rows] = hidden
        later = normalize(hidden.astype(jnp.float32), gain_mid).astype(jnp.bfloat16)
        query_ref[:, rows] = (dot(later, w_query_ref[...]) * SCALE).T.astype(jnp.bfloat16)
    for copy in copy_all([(hidden_ref, hidden_hbm), (query_ref, query_hbm)], out_sems):
        copy.wait()


def pair_rows(pair):
    return pl.ds(pl.multiple_of(128 * pair, 128), 128)


def attention(
    pick_ref, near_ref, far_ref, w_key_hbm, w_value_hbm, w_out_hbm, query_0, query_1, hidden_0,
    hidden_1, out_hbm, key_ref, value_ref, mixed_ref, w_both_ref, w_out_ref, query_ref, hidden_ref,
    out_ref, sems, out_sems,
):
    half = ROWS // 2
    moves = copy_all(
        [
            (source.at[:, pl.ds(128 * pair, 128)], w_both_ref.at[:, pl.ds(256 * pair + place, 128)])
            for pair in range(PAIRS)
            for source, place in ((w_key_hbm, 0), (w_value_hbm, 128))
        ]
        + [
            (query_0, query_ref.at[0]),
            (query_1, query_ref.at[1]),
            (w_out_hbm, w_out_ref),
            (hidden_0, hidden_ref.at[0]),
            (hidden_1, hidden_ref.at[1]),
        ],
        sems,
    )

    def context(pair, slot):
        lanes = pl.ds(pl.multiple_of(256 * pair, 256), 256)
        left = lax.broadcasted_iota(jnp.int32, (half, 128), 1) < HEAD_DIM
        for number, ctx_ref in enumerate((near_ref, far_ref)):
            rows = slice(half * number, half * number + half)
            both = dot(ctx_ref[...], w_both_ref[:, lanes])
            keys, values = both[:, :128], both[:, 128:].T.astype(jnp.bfloat16)
            for side in range(2):
                mine = left if side == 0 else ~left
                key_ref[slot, side, rows] = jnp.where(mine, keys, 0.0).astype(jnp.bfloat16)
                value_ref[slot, side, :HEAD_DIM, rows] = values[HEAD_DIM * side :][:HEAD_DIM]

    def project(frame):
        projected = dot(mixed_ref[frame].T, w_out_ref[...])
        out = (hidden_ref[frame].astype(jnp.float32) + projected).astype(jnp.bfloat16)
        out_ref[frame] = out
        place = jnp.where(pick_ref[0] == 0, frame, 1 - frame)
        return copy_all([(out_ref.at[frame], out_hbm.at[place])], out_sems.at[pl.ds(frame, 1)])

    moves, late = moves[: 2 * PAIRS], moves[2 * PAIRS :]
    value_ref[:, :, HEAD_DIM:] = jnp.ones((2, 2, ONES, ROWS), jnp.bfloat16)
    for move in moves + late[:2]:
        move.wait()
    inside = None
    context(0, 0)
    for pair in range(PAIRS):
        if pair + 1 < PAIRS:
            context(pair + 1, (pair + 1) % 2)
        for frame in range(2):
            for side in range(2):
                scores = dot(key_ref[pair % 2, side], query_ref[frame, 128 * pair : 128 * pair + 128])
                weights = jnp.exp2(scores).astype(jnp.bfloat16)
                total = dot(value_ref[pair % 2, side], weights)
                sums = total[HEAD_DIM : HEAD_DIM + 1]
                good = jnp.where((sums >= LOW) & (sums <= HIGH), 1.0, 0.0)
                inside = good if inside is None else jnp.minimum(inside, good)
                head = HEAD_DIM * (2 * pair + side)
                mixed = total[:HEAD_DIM] * (1.0 / sums)
                mixed_ref[frame, head : head + HEAD_DIM] = mixed.astype(jnp.bfloat16)
    for move in late[2:]:
        move.wait()
    writes = project(0) + project(1)
    worst = jnp.min(inside)
    for write in writes:
        write.wait()

    @pl.when(worst < 0.5)
    def _():
        def some_pixels(strip, pair):
            pixels = pl.ds(pl.multiple_of(strip * 128, 128), 128)
            for frame in range(2):
                query = query_ref[frame, pair_rows(pair), pixels]
                for side in range(2):
                    scores = dot(key_ref[0, side], query)
                    weights = jnp.exp2(scores - jnp.max(scores, 0, keepdims=True))
                    total = dot(value_ref[0, side], weights.astype(jnp.bfloat16))
                    mixed = total[:HEAD_DIM] * (1.0 / total[HEAD_DIM : HEAD_DIM + 1])
                    rows = pl.ds(pl.multiple_of(128 * pair + HEAD_DIM * side, HEAD_DIM), HEAD_DIM)
                    mixed_ref[frame, rows, pixels] = mixed.astype(jnp.bfloat16)
            return pair

        def one_pair(pair, carry):
            context(pair, 0)
            lax.fori_loop(0, PIX // 128, some_pixels, pair)
            return carry

        lax.fori_loop(0, PAIRS, one_pair, 0)
        for write in project(0) + project(1):
            write.wait()


def attend(*operands):
    frame, pair, square, half = (PIX, C), (2, PIX, C), (C, C), jnp.bfloat16
    here, there = pl.BlockSpec(memory_space=pltpu.VMEM), pl.BlockSpec(memory_space=pltpu.HBM)
    return call(
        attention,
        "attention",
        jax.ShapeDtypeStruct(pair, half),
        [pl.BlockSpec(memory_space=pltpu.SMEM), here, here] + [there] * 7,
        there,
        2 * 10**10,
        10 * 10**6,
        ATTENTION_VMEM,
        scratch_shapes=[
            pltpu.VMEM((2, 2, ROWS, 128), half),
            pltpu.VMEM((2, 2, HEAD_DIM + ONES, ROWS), half),
            pltpu.VMEM(pair, half),
            pltpu.VMEM((C, 2 * C), half),
            pltpu.VMEM(square, half),
            pltpu.VMEM(pair, half),
            pltpu.VMEM(pair, half),
            pltpu.VMEM(pair, half),
            pltpu.SemaphoreType.DMA((2 * PAIRS + 5,)),
            pltpu.SemaphoreType.DMA((2,)),
        ],
    )(*operands)


def shards(
    latents,
    timestep,
    context_frame,
    gain_pre,
    w_temporal,
    w_time,
    gain_mid,
    w_query,
    w_key,
    w_value,
    w_out,
):
    core = lax.axis_index("group") % 2
    pick = jnp.where(context_frame == 0, 0, 1)
    apart = jnp.where(pick == core, 1, 0)
    abroad = [(i, (i + 1) % 256 if i % 2 else (i - 1) % 256) for i in range(256)]
    beyond = lax.ppermute(lax.dynamic_slice_in_dim(latents, core, 1, 0), AXES, abroad)
    beside = lax.ppermute(
        lax.dynamic_slice_in_dim(latents, 1 - core, 1, 0), AXES, [(i, i ^ 1) for i in range(256)]
    )

    gain_pre = gain_pre.reshape(1, C)
    gain_mid = gain_mid.reshape(1, C)
    frame, pair, square = (PIX, C), (2, PIX, C), (C, C)
    half, single = jnp.bfloat16, jnp.float32
    mac = 2 * PIX * C * C
    here, there = pl.BlockSpec(memory_space=pltpu.VMEM), pl.BlockSpec(memory_space=pltpu.HBM)
    scalar = pl.BlockSpec(memory_space=pltpu.SMEM)
    temb = time_bias(timestep, w_time)
    soon_part, part, other_part = call(
        own_taps,
        "own_taps",
        (jax.ShapeDtypeStruct(frame, single),) * 3,
        [scalar, here, here, here, there],
        (here, here, here),
        4 * mac,
        8 * 10**6,
        TAPS_VMEM,
        scratch_shapes=[pltpu.VMEM((2 * C, 2 * C), half), pltpu.SemaphoreType.DMA((4,))],
    )(pick, latents, gain_pre, temb, w_temporal)

    row = np.arange(2 * PW)
    left = np.broadcast_to((row % PW < PW // 2)[:, None], (2 * PW, C))
    sides = jnp.asarray(np.concatenate([left, ~left], axis=1), single)
    ctx = call(
        context_rows,
        "context_rows",
        jax.ShapeDtypeStruct((32, 4, C), half),
        [scalar, scalar, here, here, here, here, here, here, here],
        here,
        mac,
        8 * 10**6,
        CONTEXT_VMEM,
    )(pick, apart, beside, beyond, gain_pre, gain_mid, sides, soon_part, w_temporal)
    def frame_call(slot, frame_part):
        return call(
            functools.partial(hidden_queries, slot),
            "hidden_queries",
            (jax.ShapeDtypeStruct(frame, half), jax.ShapeDtypeStruct(frame, half)),
            [scalar, scalar, here, here, there, there, there, there, there],
            (there, there),
            2 * mac,
            6 * 10**6,
            HIDDEN_VMEM,
            scratch_shapes=[
                pltpu.VMEM(frame, half),
                pltpu.VMEM(frame, single),
                pltpu.VMEM(square, half),
                pltpu.VMEM(square, half),
                pltpu.VMEM(frame, half),
                pltpu.VMEM(frame, half),
                pltpu.SemaphoreType.DMA((4,)),
                pltpu.SemaphoreType.DMA((2,)),
            ],
        )(pick, apart, gain_pre, gain_mid, beside, beyond, frame_part, w_temporal, w_query)

    line = exchange(ctx, groups_by(lambda x, y, z, core: (x % 2, y % 2, core))).reshape(128, C)
    hidden_0, query_0 = frame_call(0, part)
    line, hidden_0, query_0 = lax.optimization_barrier((line, hidden_0, query_0))
    near = groups_by(lambda x, y, z, core: ((x + core) % 4 // 2, (y + core) % 4 // 2, z, core))
    plane = exchange(jnp.broadcast_to(line[None], (4, 128, C)), near).reshape(512, C)
    hidden_1, query_1 = frame_call(1, other_part)
    plane, hidden_1, query_1 = lax.optimization_barrier((plane, hidden_1, query_1))
    swapped = lax.ppermute(plane, AXES, [(i, i ^ 1) for i in range(256)])

    return attend(
        pick, plane, swapped, w_key, w_value, w_out, query_0, query_1, hidden_0, hidden_1
    )


def solution(mesh):
    return jax.shard_map(
        shards,
        mesh=mesh,
        in_specs=(
            P(("clip", "group"), None, None),
            P(),
            P(("clip", "group")),
            P(),
            P(),
            P(),
            P(),
            P(),
            P(),
            P(),
            P(),
        ),
        out_specs=P(("clip", "group"), None, None),
        check_vma=False,
    )
```

```python
import functools
import math

import jax
import jax.numpy as jnp
import numpy as np
from jax import lax
from jax.experimental import pallas as pl
from jax.experimental.pallas import tpu as pltpu
from jax.sharding import PartitionSpec as P

HEAD_DIM = 64
PH = 32
PW = 20
PIX = PH * PW
C = 640
PAIRS = C // (2 * HEAD_DIM)
ROWS = 1024
ONES = 16
STRIP = 320
AXES = ("clip", "group")
MIB = 2**20
TAPS_VMEM = 24 * MIB
CONTEXT_VMEM = 24 * MIB
HIDDEN_VMEM = 56 * MIB
ATTENTION_VMEM = 52 * MIB
SCALE = math.log2(math.e) / math.sqrt(HEAD_DIM)
LOW, HIGH = 2.0**-100, 2.0**110


def place(device):
    clip, group = divmod(device, 32)
    x_low, y = divmod(clip, 4)
    x_high, rest = divmod(group, 16)
    z, core = divmod(rest, 2)
    return x_high * 2 + x_low, y, z, core


def groups_by(key):
    found = {}
    for device in range(256):
        found.setdefault(key(*place(device)), []).append(device)
    return list(found.values())


def exchange(copies, groups):
    return lax.all_to_all(copies, AXES, 0, 0, axis_index_groups=groups, tiled=False)


def dot(a, b):
    return jnp.dot(a, b, preferred_element_type=jnp.float32)


def normalize(values, gain):
    return values * lax.rsqrt(jnp.mean(values * values, -1, keepdims=True) + 1e-06) * gain


def time_bias(timestep, w_time):
    half = w_time.shape[0] // 2
    freqs = jnp.exp(-math.log(10000.0) * jnp.arange(half, dtype=jnp.float32) / half)
    angle = timestep.astype(jnp.float32)[0] * freqs
    embed = jnp.concatenate([jnp.cos(angle), jnp.sin(angle)])
    return jnp.dot(
        jax.nn.silu(embed)[None, :],
        w_time,
        precision=lax.Precision.HIGHEST,
        preferred_element_type=jnp.float32,
    )


def call(kernel, name, out_shape, in_specs, out_specs, flops, moved, vmem, **kwargs):
    return pl.pallas_call(
        kernel,
        out_shape=out_shape,
        in_specs=in_specs,
        out_specs=out_specs,
        name=name,
        compiler_params=pltpu.CompilerParams(vmem_limit_bytes=vmem),
        cost_estimate=pl.CostEstimate(flops=flops, bytes_accessed=moved, transcendentals=0),
        **kwargs,
    )


def copy_all(pairs, sems):
    copies = [pltpu.make_async_copy(a, b, sems.at[i]) for i, (a, b) in enumerate(pairs)]
    for copy in copies:
        copy.start()
    return copies


def strips():
    return [slice(start, start + STRIP) for start in range(0, PIX, STRIP)]


def own_taps(
    pick_ref, latents_ref, gain_ref, temb_ref, taps_ref, soon_ref, chosen_ref, other_ref, big_ref, sems
):
    first = pick_ref[0] == 0
    order = ((1, 0), (2, 1))
    copies = copy_all(
        [
            (taps_ref.at[order[i][j]], big_ref.at[pl.ds(C * i, C), pl.ds(C * j, C)])
            for i in range(2)
            for j in range(2)
        ],
        sems,
    )
    gain, temb = gain_ref[...], temb_ref[...]
    for copy in copies:
        copy.wait()
    for rows in strips():
        source = [latents_ref[f, rows].astype(jnp.float32) for f in range(2)]
        norm = jnp.concatenate([normalize(s, gain).astype(jnp.bfloat16) for s in source], axis=1)
        both = dot(norm, big_ref[...])
        parts = [source[f] + temb + both[:, C * f : C * f + C] for f in range(2)]
        chosen = jnp.where(first, parts[0], parts[1])
        soon_ref[rows] = chosen
        chosen_ref[rows] = chosen
        other_ref[rows] = jnp.where(first, parts[1], parts[0])


def context_rows(
    pick_ref, apart_ref, beside_ref, beyond_ref, gain_pre_ref, gain_mid_ref, side_ref, part_ref,
    taps_ref, ctx_ref,
):
    tap = jnp.where(pick_ref[0] == 0, 0, 2)
    far = apart_ref[0] == 1
    gain_pre, gain_mid = gain_pre_ref[...], gain_mid_ref[...]
    tile = side_ref.shape[0]
    sums = []
    for half in range(2):
        rows = slice(half * PIX // 2, (half + 1) * PIX // 2)
        halo = jnp.where(far, beyond_ref[0, rows], beside_ref[0, rows]).astype(jnp.float32)
        norm = normalize(halo, gain_pre).astype(jnp.bfloat16)
        hidden = (part_ref[rows] + dot(norm, taps_ref[tap])).astype(jnp.bfloat16)
        norm = normalize(hidden.astype(jnp.float32), gain_mid).astype(jnp.bfloat16)
        norm = norm.astype(jnp.float32).reshape(PIX // 2 // tile, tile, C)
        for side in range(2):
            here = jnp.sum(norm * side_ref[:, C * side : C * side + C], axis=0)
            sums.append(jnp.sum(here, axis=0, keepdims=True))
    pooled = jnp.concatenate(sums, axis=0) * (4.0 / PIX)
    rows = normalize(pooled, 1.0).astype(jnp.bfloat16)
    for copy in range(ctx_ref.shape[0]):
        ctx_ref[copy] = rows


def hidden_queries(
    pick_ref, apart_ref, gain_pre_ref, gain_mid_ref, beside_hbm, beyond_hbm, part_hbm, other_part_hbm,
    taps_hbm, w_query_hbm, hidden_0, hidden_1, query_0, query_1, halo_ref, part_ref, tap_ref,
    w_query_ref, hidden_ref, query_ref, sems, halo_sems, out_sems,
):
    loads = []
    for slot, part in enumerate((part_hbm, other_part_hbm)):
        far = (apart_ref[0] == 1) == (slot == 0)
        tap = jnp.where((pick_ref[0] == 0) == (slot == 0), 0, 2)
        place = halo_ref.at[slot]
        halo_copy = pltpu.make_async_copy(beyond_hbm.at[0], place, halo_sems.at[slot])
        pl.when(far)(halo_copy.start)
        pl.when(~far)(pltpu.make_async_copy(beside_hbm.at[0], place, halo_sems.at[slot]).start)
        pairs = [(taps_hbm.at[tap], tap_ref.at[slot]), (part, part_ref.at[slot])]
        if slot == 0:
            pairs.append((w_query_hbm, w_query_ref))
        loads.append([halo_copy] + copy_all(pairs, sems.at[pl.ds(3 * slot, 3 - slot)]))
    gain_pre, gain_mid = gain_pre_ref[...], gain_mid_ref[...]
    writes = []
    for slot, (hidden_out, query_out) in enumerate(((hidden_0, query_0), (hidden_1, query_1))):
        for load in loads[slot]:
            load.wait()
        norm = normalize(halo_ref[slot].astype(jnp.float32), gain_pre).astype(jnp.bfloat16)
        hidden = (part_ref[slot] + dot(norm, tap_ref[slot])).astype(jnp.bfloat16)
        hidden_ref[slot] = hidden
        norm = normalize(hidden.astype(jnp.float32), gain_mid).astype(jnp.bfloat16)
        query_ref[slot] = (dot(norm, w_query_ref[...]) * SCALE).T.astype(jnp.bfloat16)
        writes += copy_all(
            [(hidden_ref.at[slot], hidden_out), (query_ref.at[slot], query_out)],
            out_sems.at[pl.ds(2 * slot, 2)],
        )
    for write in writes:
        write.wait()


def pair_rows(pair):
    return pl.ds(pl.multiple_of(128 * pair, 128), 128)


def attention(
    pick_ref, near_ref, far_ref, w_key_hbm, w_value_hbm, w_out_hbm, query_0, query_1, hidden_0,
    hidden_1, out_hbm, key_ref, value_ref, mixed_ref, w_both_ref, w_out_ref, query_ref, hidden_ref,
    out_ref, sems, out_sems,
):
    half = ROWS // 2
    moves = copy_all(
        [
            (source.at[:, pl.ds(128 * pair, 128)], w_both_ref.at[:, pl.ds(256 * pair + place, 128)])
            for pair in range(PAIRS)
            for source, place in ((w_key_hbm, 0), (w_value_hbm, 128))
        ]
        + [
            (query_0, query_ref.at[0]),
            (query_1, query_ref.at[1]),
            (w_out_hbm, w_out_ref),
            (hidden_0, hidden_ref.at[0]),
            (hidden_1, hidden_ref.at[1]),
        ],
        sems,
    )

    def context(pair, slot):
        lanes = pl.ds(pl.multiple_of(256 * pair, 256), 256)
        left = lax.broadcasted_iota(jnp.int32, (half, 128), 1) < HEAD_DIM
        for number, ctx_ref in enumerate((near_ref, far_ref)):
            rows = slice(half * number, half * number + half)
            both = dot(ctx_ref[...], w_both_ref[:, lanes])
            keys, values = both[:, :128], both[:, 128:].T.astype(jnp.bfloat16)
            for side in range(2):
                mine = left if side == 0 else ~left
                key_ref[slot, side, rows] = jnp.where(mine, keys, 0.0).astype(jnp.bfloat16)
                value_ref[slot, side, :HEAD_DIM, rows] = values[HEAD_DIM * side :][:HEAD_DIM]

    def project(frame):
        projected = dot(mixed_ref[frame].T, w_out_ref[...])
        out = (hidden_ref[frame].astype(jnp.float32) + projected).astype(jnp.bfloat16)
        out_ref[frame] = out
        place = jnp.where(pick_ref[0] == 0, frame, 1 - frame)
        return copy_all([(out_ref.at[frame], out_hbm.at[place])], out_sems.at[pl.ds(frame, 1)])

    moves, late = moves[: 2 * PAIRS], moves[2 * PAIRS :]
    value_ref[:, :, HEAD_DIM:] = jnp.ones((2, 2, ONES, ROWS), jnp.bfloat16)
    for move in moves + late[:2]:
        move.wait()
    inside = None
    context(0, 0)
    for pair in range(PAIRS):
        if pair + 1 < PAIRS:
            context(pair + 1, (pair + 1) % 2)
        for frame in range(2):
            for side in range(2):
                scores = dot(key_ref[pair % 2, side], query_ref[frame, 128 * pair : 128 * pair + 128])
                weights = jnp.exp2(scores).astype(jnp.bfloat16)
                total = dot(value_ref[pair % 2, side], weights)
                sums = total[HEAD_DIM : HEAD_DIM + 1]
                good = jnp.where((sums >= LOW) & (sums <= HIGH), 1.0, 0.0)
                inside = good if inside is None else jnp.minimum(inside, good)
                head = HEAD_DIM * (2 * pair + side)
                mixed = total[:HEAD_DIM] * (1.0 / sums)
                mixed_ref[frame, head : head + HEAD_DIM] = mixed.astype(jnp.bfloat16)
    for move in late[2:]:
        move.wait()
    writes = project(0) + project(1)
    worst = jnp.min(inside)
    for write in writes:
        write.wait()

    @pl.when(worst < 0.5)
    def _():
        def some_pixels(strip, pair):
            pixels = pl.ds(pl.multiple_of(strip * 128, 128), 128)
            for frame in range(2):
                query = query_ref[frame, pair_rows(pair), pixels]
                for side in range(2):
                    scores = dot(key_ref[0, side], query)
                    weights = jnp.exp2(scores - jnp.max(scores, 0, keepdims=True))
                    total = dot(value_ref[0, side], weights.astype(jnp.bfloat16))
                    mixed = total[:HEAD_DIM] * (1.0 / total[HEAD_DIM : HEAD_DIM + 1])
                    rows = pl.ds(pl.multiple_of(128 * pair + HEAD_DIM * side, HEAD_DIM), HEAD_DIM)
                    mixed_ref[frame, rows, pixels] = mixed.astype(jnp.bfloat16)
            return pair

        def one_pair(pair, carry):
            context(pair, 0)
            lax.fori_loop(0, PIX // 128, some_pixels, pair)
            return carry

        lax.fori_loop(0, PAIRS, one_pair, 0)
        for write in project(0) + project(1):
            write.wait()


def attend(*operands):
    frame, pair, square, half = (PIX, C), (2, PIX, C), (C, C), jnp.bfloat16
    here, there = pl.BlockSpec(memory_space=pltpu.VMEM), pl.BlockSpec(memory_space=pltpu.HBM)
    return call(
        attention,
        "attention",
        jax.ShapeDtypeStruct(pair, half),
        [pl.BlockSpec(memory_space=pltpu.SMEM), here, here] + [there] * 7,
        there,
        2 * 10**10,
        10 * 10**6,
        ATTENTION_VMEM,
        scratch_shapes=[
            pltpu.VMEM((2, 2, ROWS, 128), half),
            pltpu.VMEM((2, 2, HEAD_DIM + ONES, ROWS), half),
            pltpu.VMEM(pair, half),
            pltpu.VMEM((C, 2 * C), half),
            pltpu.VMEM(square, half),
            pltpu.VMEM(pair, half),
            pltpu.VMEM(pair, half),
            pltpu.VMEM(pair, half),
            pltpu.SemaphoreType.DMA((2 * PAIRS + 5,)),
            pltpu.SemaphoreType.DMA((2,)),
        ],
    )(*operands)


def shards(
    latents,
    timestep,
    context_frame,
    gain_pre,
    w_temporal,
    w_time,
    gain_mid,
    w_query,
    w_key,
    w_value,
    w_out,
):
    core = lax.axis_index("group") % 2
    pick = jnp.where(context_frame == 0, 0, 1)
    apart = jnp.where(pick == core, 1, 0)
    abroad = [(i, (i + 1) % 256 if i % 2 else (i - 1) % 256) for i in range(256)]
    beyond = lax.ppermute(lax.dynamic_slice_in_dim(latents, core, 1, 0), AXES, abroad)
    beside = lax.ppermute(
        lax.dynamic_slice_in_dim(latents, 1 - core, 1, 0), AXES, [(i, i ^ 1) for i in range(256)]
    )

    gain_pre = gain_pre.reshape(1, C)
    gain_mid = gain_mid.reshape(1, C)
    frame, pair, square = (PIX, C), (2, PIX, C), (C, C)
    half, single = jnp.bfloat16, jnp.float32
    mac = 2 * PIX * C * C
    here, there = pl.BlockSpec(memory_space=pltpu.VMEM), pl.BlockSpec(memory_space=pltpu.HBM)
    scalar = pl.BlockSpec(memory_space=pltpu.SMEM)
    temb = time_bias(timestep, w_time)
    soon_part, part, other_part = call(
        own_taps,
        "own_taps",
        (jax.ShapeDtypeStruct(frame, single),) * 3,
        [scalar, here, here, here, there],
        (here, here, here),
        4 * mac,
        8 * 10**6,
        TAPS_VMEM,
        scratch_shapes=[pltpu.VMEM((2 * C, 2 * C), half), pltpu.SemaphoreType.DMA((4,))],
    )(pick, latents, gain_pre, temb, w_temporal)

    row = np.arange(2 * PW)
    left = np.broadcast_to((row % PW < PW // 2)[:, None], (2 * PW, C))
    sides = jnp.asarray(np.concatenate([left, ~left], axis=1), single)
    ctx = call(
        context_rows,
        "context_rows",
        jax.ShapeDtypeStruct((8, 4, C), half),
        [scalar, scalar, here, here, here, here, here, here, here],
        here,
        mac,
        8 * 10**6,
        CONTEXT_VMEM,
    )(pick, apart, beside, beyond, gain_pre, gain_mid, sides, soon_part, w_temporal)
    hidden_0, hidden_1, query_0, query_1 = call(
        hidden_queries,
        "hidden_queries",
        (jax.ShapeDtypeStruct(frame, half),) * 4,
        [scalar, scalar, here, here] + [there] * 6,
        (there,) * 4,
        4 * mac,
        12 * 10**6,
        HIDDEN_VMEM,
        scratch_shapes=[
            pltpu.VMEM(pair, half),
            pltpu.VMEM(pair, single),
            pltpu.VMEM(pair, half),
            pltpu.VMEM(square, half),
            pltpu.VMEM(pair, half),
            pltpu.VMEM(pair, half),
            pltpu.SemaphoreType.DMA((5,)),
            pltpu.SemaphoreType.DMA((2,)),
            pltpu.SemaphoreType.DMA((4,)),
        ],
    )(pick, apart, gain_pre, gain_mid, beside, beyond, part, other_part, w_temporal, w_query)

    line = exchange(ctx, groups_by(lambda x, y, z, core: (x, y, core))).reshape(32, C)
    plane = exchange(
        jnp.broadcast_to(line[None], (16, 32, C)), groups_by(lambda x, y, z, core: (z, core))
    ).reshape(512, C)
    plane, hidden_0, hidden_1, query_0, query_1 = lax.optimization_barrier(
        (plane, hidden_0, hidden_1, query_0, query_1)
    )
    swapped = lax.ppermute(plane, AXES, [(i, i ^ 1) for i in range(256)])

    return attend(
        pick, plane, swapped, w_key, w_value, w_out, query_0, query_1, hidden_0, hidden_1
    )


def solution(mesh):
    return jax.shard_map(
        shards,
        mesh=mesh,
        in_specs=(
            P(("clip", "group"), None, None),
            P(),
            P(("clip", "group")),
            P(),
            P(),
            P(),
            P(),
            P(),
            P(),
            P(),
            P(),
        ),
        out_specs=P(("clip", "group"), None, None),
        check_vma=False,
    )
```

```python
import functools
import math

import jax
import jax.numpy as jnp
import numpy as np
from jax import lax
from jax.experimental import pallas as pl
from jax.experimental.pallas import tpu as pltpu
from jax.sharding import PartitionSpec as P

HEAD_DIM = 64
PH = 32
PW = 20
PIX = PH * PW
C = 640
PAIRS = C // (2 * HEAD_DIM)
ROWS = 1024
ONES = 16
STRIP = 320
AXES = ("clip", "group")
MIB = 2**20
TAPS_VMEM = 24 * MIB
CONTEXT_VMEM = 24 * MIB
HIDDEN_VMEM = 56 * MIB
ATTENTION_VMEM = 52 * MIB
SCALE = math.log2(math.e) / math.sqrt(HEAD_DIM)
LOW, HIGH = 2.0**-100, 2.0**110


def place(device):
    clip, group = divmod(device, 32)
    x_low, y = divmod(clip, 4)
    x_high, rest = divmod(group, 16)
    z, core = divmod(rest, 2)
    return x_high * 2 + x_low, y, z, core


def groups_by(key):
    found = {}
    for device in range(256):
        found.setdefault(key(*place(device)), []).append(device)
    return list(found.values())


def exchange(copies, groups):
    return lax.all_to_all(copies, AXES, 0, 0, axis_index_groups=groups, tiled=False)


def dot(a, b):
    return jnp.dot(a, b, preferred_element_type=jnp.float32)


def normalize(values, gain):
    return values * lax.rsqrt(jnp.mean(values * values, -1, keepdims=True) + 1e-06) * gain


def time_bias(timestep, w_time):
    half = w_time.shape[0] // 2
    freqs = jnp.exp(-math.log(10000.0) * jnp.arange(half, dtype=jnp.float32) / half)
    angle = timestep.astype(jnp.float32)[0] * freqs
    embed = jnp.concatenate([jnp.cos(angle), jnp.sin(angle)])
    return jnp.dot(
        jax.nn.silu(embed)[None, :],
        w_time,
        precision=lax.Precision.HIGHEST,
        preferred_element_type=jnp.float32,
    )


def call(kernel, name, out_shape, in_specs, out_specs, flops, moved, vmem, **kwargs):
    return pl.pallas_call(
        kernel,
        out_shape=out_shape,
        in_specs=in_specs,
        out_specs=out_specs,
        name=name,
        compiler_params=pltpu.CompilerParams(vmem_limit_bytes=vmem),
        cost_estimate=pl.CostEstimate(flops=flops, bytes_accessed=moved, transcendentals=0),
        **kwargs,
    )


def copy_all(pairs, sems):
    copies = [pltpu.make_async_copy(a, b, sems.at[i]) for i, (a, b) in enumerate(pairs)]
    for copy in copies:
        copy.start()
    return copies


def strips():
    return [slice(start, start + STRIP) for start in range(0, PIX, STRIP)]


def own_taps(
    pick_ref, latents_ref, gain_ref, temb_ref, taps_ref, soon_ref, chosen_ref, other_ref, big_ref, sems
):
    first = pick_ref[0] == 0
    order = ((1, 0), (2, 1))
    copies = copy_all(
        [
            (taps_ref.at[order[i][j]], big_ref.at[pl.ds(C * i, C), pl.ds(C * j, C)])
            for i in range(2)
            for j in range(2)
        ],
        sems,
    )
    gain, temb = gain_ref[...], temb_ref[...]
    for copy in copies:
        copy.wait()
    for rows in strips():
        source = [latents_ref[f, rows].astype(jnp.float32) for f in range(2)]
        norm = jnp.concatenate([normalize(s, gain).astype(jnp.bfloat16) for s in source], axis=1)
        both = dot(norm, big_ref[...])
        parts = [source[f] + temb + both[:, C * f : C * f + C] for f in range(2)]
        chosen = jnp.where(first, parts[0], parts[1])
        soon_ref[rows] = chosen
        chosen_ref[rows] = chosen
        other_ref[rows] = jnp.where(first, parts[1], parts[0])


def context_rows(
    pick_ref, apart_ref, beside_ref, beyond_ref, gain_pre_ref, gain_mid_ref, side_ref, part_ref,
    taps_ref, ctx_ref,
):
    tap = jnp.where(pick_ref[0] == 0, 0, 2)
    far = apart_ref[0] == 1
    gain_pre, gain_mid = gain_pre_ref[...], gain_mid_ref[...]
    tile = side_ref.shape[0]
    sums = []
    for half in range(2):
        rows = slice(half * PIX // 2, (half + 1) * PIX // 2)
        halo = jnp.where(far, beyond_ref[0, rows], beside_ref[0, rows]).astype(jnp.float32)
        norm = normalize(halo, gain_pre).astype(jnp.bfloat16)
        hidden = (part_ref[rows] + dot(norm, taps_ref[tap])).astype(jnp.bfloat16)
        norm = normalize(hidden.astype(jnp.float32), gain_mid).astype(jnp.bfloat16)
        norm = norm.astype(jnp.float32).reshape(PIX // 2 // tile, tile, C)
        for side in range(2):
            here = jnp.sum(norm * side_ref[:, C * side : C * side + C], axis=0)
            sums.append(jnp.sum(here, axis=0, keepdims=True))
    pooled = jnp.concatenate(sums, axis=0) * (4.0 / PIX)
    rows = normalize(pooled, 1.0).astype(jnp.bfloat16)
    for copy in range(ctx_ref.shape[0]):
        ctx_ref[copy] = rows


def hidden_queries(
    pick_ref, apart_ref, gain_pre_ref, gain_mid_ref, beside_hbm, beyond_hbm, part_hbm, other_part_hbm,
    taps_hbm, w_query_hbm, hidden_0, hidden_1, query_0, query_1, halo_ref, part_ref, tap_ref,
    w_query_ref, hidden_ref, query_ref, sems, halo_sems, out_sems,
):
    loads = []
    for slot, part in enumerate((part_hbm, other_part_hbm)):
        far = (apart_ref[0] == 1) == (slot == 0)
        tap = jnp.where((pick_ref[0] == 0) == (slot == 0), 0, 2)
        place = halo_ref.at[slot]
        halo_copy = pltpu.make_async_copy(beyond_hbm.at[0], place, halo_sems.at[slot])
        pl.when(far)(halo_copy.start)
        pl.when(~far)(pltpu.make_async_copy(beside_hbm.at[0], place, halo_sems.at[slot]).start)
        pairs = [(taps_hbm.at[tap], tap_ref.at[slot]), (part, part_ref.at[slot])]
        if slot == 0:
            pairs.append((w_query_hbm, w_query_ref))
        loads.append([halo_copy] + copy_all(pairs, sems.at[pl.ds(3 * slot, 3 - slot)]))
    gain_pre, gain_mid = gain_pre_ref[...], gain_mid_ref[...]
    writes = []
    for slot, (hidden_out, query_out) in enumerate(((hidden_0, query_0), (hidden_1, query_1))):
        for load in loads[slot]:
            load.wait()
        norm = normalize(halo_ref[slot].astype(jnp.float32), gain_pre).astype(jnp.bfloat16)
        hidden = (part_ref[slot] + dot(norm, tap_ref[slot])).astype(jnp.bfloat16)
        hidden_ref[slot] = hidden
        norm = normalize(hidden.astype(jnp.float32), gain_mid).astype(jnp.bfloat16)
        query_ref[slot] = (dot(norm, w_query_ref[...]) * SCALE).T.astype(jnp.bfloat16)
        writes += copy_all(
            [(hidden_ref.at[slot], hidden_out), (query_ref.at[slot], query_out)],
            out_sems.at[pl.ds(2 * slot, 2)],
        )
    for write in writes:
        write.wait()


def pair_rows(pair):
    return pl.ds(pl.multiple_of(128 * pair, 128), 128)


def attention(
    pick_ref, near_ref, far_ref, w_key_hbm, w_value_hbm, w_out_hbm, query_0, query_1, hidden_0,
    hidden_1, out_hbm, key_ref, value_ref, mixed_ref, w_both_ref, w_out_ref, query_ref, hidden_ref,
    out_ref, sems, out_sems,
):
    half = ROWS // 2
    weights_in = copy_all(
        [
            (source.at[:, pl.ds(128 * pair, 128)], w_both_ref.at[:, pl.ds(256 * pair + place, 128)])
            for pair in range(PAIRS)
            for source, place in ((w_key_hbm, 0), (w_value_hbm, 128))
        ],
        sems.at[pl.ds(0, 2 * PAIRS)],
    )
    queries_in = copy_all(
        [(query_0, query_ref.at[0]), (query_1, query_ref.at[1])], sems.at[pl.ds(2 * PAIRS, 2)]
    )

    def context(pair, slot):
        lanes = pl.ds(pl.multiple_of(256 * pair, 256), 256)
        left = lax.broadcasted_iota(jnp.int32, (half, 128), 1) < HEAD_DIM
        for number, ctx_ref in enumerate((near_ref, far_ref)):
            rows = slice(half * number, half * number + half)
            both = dot(ctx_ref[...], w_both_ref[:, lanes])
            keys, values = both[:, :128], both[:, 128:].T.astype(jnp.bfloat16)
            for side in range(2):
                mine = left if side == 0 else ~left
                key_ref[slot, side, rows] = jnp.where(mine, keys, 0.0).astype(jnp.bfloat16)
                value_ref[slot, side, :HEAD_DIM, rows] = values[HEAD_DIM * side :][:HEAD_DIM]

    def project(frame):
        projected = dot(mixed_ref[frame].T, w_out_ref[...])
        out = (hidden_ref[frame].astype(jnp.float32) + projected).astype(jnp.bfloat16)
        out_ref[frame] = out
        place = jnp.where(pick_ref[0] == 0, frame, 1 - frame)
        return copy_all([(out_ref.at[frame], out_hbm.at[place])], out_sems.at[pl.ds(frame, 1)])

    value_ref[:, :, HEAD_DIM:] = jnp.ones((2, 2, ONES, ROWS), jnp.bfloat16)
    for move in weights_in[:2]:
        move.wait()
    context(0, 0)
    for move in weights_in[2:] + queries_in:
        move.wait()
    late = copy_all(
        [
            (w_out_hbm, w_out_ref),
            (hidden_0, hidden_ref.at[0]),
            (hidden_1, hidden_ref.at[1]),
        ],
        sems.at[pl.ds(2 * PAIRS + 2, 3)],
    )
    inside = None
    for pair in range(PAIRS):
        if pair + 1 < PAIRS:
            context(pair + 1, (pair + 1) % 2)
        for frame in range(2):
            for side in range(2):
                scores = dot(key_ref[pair % 2, side], query_ref[frame, 128 * pair : 128 * pair + 128])
                weights = jnp.exp2(scores).astype(jnp.bfloat16)
                total = dot(value_ref[pair % 2, side], weights)
                sums = total[HEAD_DIM : HEAD_DIM + 1]
                good = jnp.where((sums >= LOW) & (sums <= HIGH), 1.0, 0.0)
                inside = good if inside is None else jnp.minimum(inside, good)
                head = HEAD_DIM * (2 * pair + side)
                mixed = total[:HEAD_DIM] * (1.0 / sums)
                mixed_ref[frame, head : head + HEAD_DIM] = mixed.astype(jnp.bfloat16)
    for move in late:
        move.wait()
    writes = project(0) + project(1)
    worst = jnp.min(inside)
    for write in writes:
        write.wait()

    @pl.when(worst < 0.5)
    def _():
        def some_pixels(strip, pair):
            pixels = pl.ds(pl.multiple_of(strip * 128, 128), 128)
            for frame in range(2):
                query = query_ref[frame, pair_rows(pair), pixels]
                for side in range(2):
                    scores = dot(key_ref[0, side], query)
                    weights = jnp.exp2(scores - jnp.max(scores, 0, keepdims=True))
                    total = dot(value_ref[0, side], weights.astype(jnp.bfloat16))
                    mixed = total[:HEAD_DIM] * (1.0 / total[HEAD_DIM : HEAD_DIM + 1])
                    rows = pl.ds(pl.multiple_of(128 * pair + HEAD_DIM * side, HEAD_DIM), HEAD_DIM)
                    mixed_ref[frame, rows, pixels] = mixed.astype(jnp.bfloat16)
            return pair

        def one_pair(pair, carry):
            context(pair, 0)
            lax.fori_loop(0, PIX // 128, some_pixels, pair)
            return carry

        lax.fori_loop(0, PAIRS, one_pair, 0)
        for write in project(0) + project(1):
            write.wait()


def attend(*operands):
    frame, pair, square, half = (PIX, C), (2, PIX, C), (C, C), jnp.bfloat16
    here, there = pl.BlockSpec(memory_space=pltpu.VMEM), pl.BlockSpec(memory_space=pltpu.HBM)
    return call(
        attention,
        "attention",
        jax.ShapeDtypeStruct(pair, half),
        [pl.BlockSpec(memory_space=pltpu.SMEM), here, here] + [there] * 7,
        there,
        2 * 10**10,
        10 * 10**6,
        ATTENTION_VMEM,
        scratch_shapes=[
            pltpu.VMEM((2, 2, ROWS, 128), half),
            pltpu.VMEM((2, 2, HEAD_DIM + ONES, ROWS), half),
            pltpu.VMEM(pair, half),
            pltpu.VMEM((C, 2 * C), half),
            pltpu.VMEM(square, half),
            pltpu.VMEM(pair, half),
            pltpu.VMEM(pair, half),
            pltpu.VMEM(pair, half),
            pltpu.SemaphoreType.DMA((2 * PAIRS + 5,)),
            pltpu.SemaphoreType.DMA((2,)),
        ],
    )(*operands)


def shards(
    latents,
    timestep,
    context_frame,
    gain_pre,
    w_temporal,
    w_time,
    gain_mid,
    w_query,
    w_key,
    w_value,
    w_out,
):
    core = lax.axis_index("group") % 2
    pick = jnp.where(context_frame == 0, 0, 1)
    apart = jnp.where(pick == core, 1, 0)
    abroad = [(i, (i + 1) % 256 if i % 2 else (i - 1) % 256) for i in range(256)]
    beyond = lax.ppermute(lax.dynamic_slice_in_dim(latents, core, 1, 0), AXES, abroad)
    beside = lax.ppermute(
        lax.dynamic_slice_in_dim(latents, 1 - core, 1, 0), AXES, [(i, i ^ 1) for i in range(256)]
    )

    gain_pre = gain_pre.reshape(1, C)
    gain_mid = gain_mid.reshape(1, C)
    frame, pair, square = (PIX, C), (2, PIX, C), (C, C)
    half, single = jnp.bfloat16, jnp.float32
    mac = 2 * PIX * C * C
    here, there = pl.BlockSpec(memory_space=pltpu.VMEM), pl.BlockSpec(memory_space=pltpu.HBM)
    scalar = pl.BlockSpec(memory_space=pltpu.SMEM)
    temb = time_bias(timestep, w_time)
    soon_part, part, other_part = call(
        own_taps,
        "own_taps",
        (jax.ShapeDtypeStruct(frame, single),) * 3,
        [scalar, here, here, here, there],
        (here, here, here),
        4 * mac,
        8 * 10**6,
        TAPS_VMEM,
        scratch_shapes=[pltpu.VMEM((2 * C, 2 * C), half), pltpu.SemaphoreType.DMA((4,))],
    )(pick, latents, gain_pre, temb, w_temporal)

    row = np.arange(2 * PW)
    left = np.broadcast_to((row % PW < PW // 2)[:, None], (2 * PW, C))
    sides = jnp.asarray(np.concatenate([left, ~left], axis=1), single)
    ctx = call(
        context_rows,
        "context_rows",
        jax.ShapeDtypeStruct((8, 4, C), half),
        [scalar, scalar, here, here, here, here, here, here, here],
        here,
        mac,
        8 * 10**6,
        CONTEXT_VMEM,
    )(pick, apart, beside, beyond, gain_pre, gain_mid, sides, soon_part, w_temporal)
    hidden_0, hidden_1, query_0, query_1 = call(
        hidden_queries,
        "hidden_queries",
        (jax.ShapeDtypeStruct(frame, half),) * 4,
        [scalar, scalar, here, here] + [there] * 6,
        (there,) * 4,
        4 * mac,
        12 * 10**6,
        HIDDEN_VMEM,
        scratch_shapes=[
            pltpu.VMEM(pair, half),
            pltpu.VMEM(pair, single),
            pltpu.VMEM(pair, half),
            pltpu.VMEM(square, half),
            pltpu.VMEM(pair, half),
            pltpu.VMEM(pair, half),
            pltpu.SemaphoreType.DMA((5,)),
            pltpu.SemaphoreType.DMA((2,)),
            pltpu.SemaphoreType.DMA((4,)),
        ],
    )(pick, apart, gain_pre, gain_mid, beside, beyond, part, other_part, w_temporal, w_query)

    line = exchange(ctx, groups_by(lambda x, y, z, core: (x, y, core))).reshape(32, C)
    plane = exchange(
        jnp.broadcast_to(line[None], (16, 32, C)), groups_by(lambda x, y, z, core: (z, core))
    ).reshape(512, C)
    plane, hidden_0, hidden_1, query_0, query_1 = lax.optimization_barrier(
        (plane, hidden_0, hidden_1, query_0, query_1)
    )
    swapped = lax.ppermute(plane, AXES, [(i, i ^ 1) for i in range(256)])

    return attend(
        pick, plane, swapped, w_key, w_value, w_out, query_0, query_1, hidden_0, hidden_1
    )


def solution(mesh):
    return jax.shard_map(
        shards,
        mesh=mesh,
        in_specs=(
            P(("clip", "group"), None, None),
            P(),
            P(("clip", "group")),
            P(),
            P(),
            P(),
            P(),
            P(),
            P(),
            P(),
            P(),
        ),
        out_specs=P(("clip", "group"), None, None),
        check_vma=False,
    )
```
